32 devices in a mesh: pair: 4 (over z), bulk: 8 (over y, x, core).
Axes of the slice: x: 2, y: 2, z: 4, core: 2. Of those that a mesh axis runs over, the one named last changes fastest.
Arguments:
- wavefield_now: float32 [128, 96, 128], P(('pair', 'bulk')), may hold values from -6 to 6
- wavefield_vel: float32 [128, 96, 128], P(('pair', 'bulk')), may hold values from -6 to 6
- speed_sq: float32 [32, 24, 32], P(('pair', 'bulk')), may hold values from 0.5 to 2
- source_field: float32 [128, 96, 128], P(('pair', 'bulk')), may hold values from -300 to 300
- wavelet: float32 [6], replicated, may hold values from -4 to 4
- slot_elem: int32 [4096], P(('pair', 'bulk')), may hold values from 0 to 767
- slot_station: int32 [4096], replicated, may hold values from 0 to 2048, as said below
- slot_weight: float32 [125, 4096], P(None, ('pair', 'bulk')), may hold values from -0.5 to 0.5
- pair_blocks: int32 [32, 2], P(('pair', 'bulk')), may hold values from 0 to 63
Outputs:
- wavefield_end: float32 [128, 96, 128], P(('pair', 'bulk'))
- cross: bfloat16 [32, 2, 256, 1024], P(('pair', 'bulk'))
The draws below stay inside these ranges and needn't reach their ends.
Inputs may be any that keep to these rules, and one draw needn't show every extreme that they name: `slot_station`: every station number 0 .. 2047 appears in exactly one slot; empty slots hold 2048. Within each device block of 128 slots the live slots come first; some device block is full in every draw. `slot_elem`: index of the slot's element within the slot block's elements. `pair_blocks`: block k holds stations k * 32 to k * 32 + 31.
All inputs are finite; a program needn't handle non-finite values.
Results may differ from the reference program's by a relative error of at most 0.0057.
Values may be sent and summed in bfloat16 or wider, within the bound.
A program may use at most 128 MiB of HBM per device.

```python
import math
import jax
import jax.numpy as jnp
import numpy as np
from jax import lax

EX_DEV = 1
EY = 24
EZ = 32
NT = 6
F = 256
STA_DEV = 64
SB = 32
CAP = 128
NSTA = 2048
NSB = 64
NPAIRS = 32
EXT = 32
NX = 128
NYN = 96
NZN = 128
DEVICES = 32


def draw_slot_station(key, part):
    key_load = jax.random.fold_in(key, 11)
    key_ids = jax.random.fold_in(key, 12)
    kinds = jnp.arange(DEVICES, dtype=jnp.int32) % 4
    loads = jnp.where(kinds == 0, CAP, jnp.where(kinds == 1, STA_DEV, STA_DEV // 2)).astype(jnp.int32)
    loads = loads[jax.random.permutation(key_load, DEVICES)]
    live_slot = (jnp.arange(CAP, dtype=jnp.int32)[None, :] < loads[:, None]).reshape(-1)
    slot_rank = jnp.cumsum(live_slot.astype(jnp.int32)) - 1
    stations = jax.random.permutation(key_ids, NSTA).astype(jnp.int32)
    return jnp.where(live_slot, stations[jnp.clip(slot_rank, 0, NSTA - 1)], NSTA).astype(jnp.int32)


def set_ends(drawn, key, least, high):
    place = [jax.random.randint(jax.random.fold_in(key, axis), (), 0, length) for axis, length in enumerate(drawn.shape)]
    widest = drawn.shape.index(max(drawn.shape))
    beside = place[:widest] + [(place[widest] + 1) % drawn.shape[widest]] + place[widest + 1:]
    return drawn.at[tuple(place)].set(least).at[tuple(beside)].set(high)


def level_of(rng, extent, cuts, least, largest):
    level, own = 1.0, jax.random.fold_in(rng, 6)
    for dim, blocks in cuts:
        heights = jnp.exp(jax.random.uniform(jax.random.fold_in(own, dim), (blocks,), jnp.float32, least / len(cuts), largest / len(cuts)))
        level = level * jnp.repeat(heights, extent[dim] // blocks).reshape([-1 if axis == dim else 1 for axis in range(len(extent))])
    return level


def bell_draw(own_key, shape, deviation, reach, shards=(), held_as=jnp.bfloat16):
    gain = level_of(own_key, shape, shards, -0.22, 0.18) if shards else 1.0
    values = jax.random.normal(own_key, shape, jnp.float32) * deviation * gain
    return jnp.minimum(jnp.maximum(values, -reach), reach).astype(held_as)


def setup_inputs(seed: int = 0) -> dict:
    streams_of = jax.random.split(jax.random.key(seed), 10)
    return {
        "wavefield_now": bell_draw(streams_of[0], (NX, NYN, NZN), 1.0, 6.0, ((0, 32),), jnp.float32),
        "wavefield_vel": bell_draw(streams_of[1], (NX, NYN, NZN), 1.0, 6.0, ((0, 32),), jnp.float32),
        "speed_sq": jnp.clip(jnp.exp(math.log(2.0) - 1.3862944 * jax.random.uniform(streams_of[2], (EXT, EY, EZ), jnp.float32) ** level_of(streams_of[2], (EXT, EY, EZ), ((0, 32),), -0.2, 0.2)), 0.5, 2.0),
        "source_field": bell_draw(streams_of[3], (NX, NYN, NZN), 50.0, 300.0, ((0, 32),), jnp.float32),
        "wavelet": bell_draw(streams_of[4], (NT,), 1.0, 4.0, (), jnp.float32),
        "slot_elem": set_ends(jax.random.randint(streams_of[5], (CAP * DEVICES,), 0, EX_DEV * EY * EZ), jax.random.fold_in(streams_of[5], 1), 0, (EX_DEV * EY * EZ) - 1).astype(jnp.int32),
        "slot_station": draw_slot_station(jax.random.fold_in(streams_of[9], 71), 0),
        "slot_weight": bell_draw(streams_of[7], (125, CAP * DEVICES), 125 ** -0.5, 0.5, ((1, 32),), jnp.float32),
        "pair_blocks": set_ends(jax.random.randint(streams_of[8], (NPAIRS, 2), 0, NSB), jax.random.fold_in(streams_of[8], 1), 0, NSB - 1).astype(jnp.int32),
    }


STEP_DT = 0.04

def gll_tables():
    points = np.array([-1.0, -math.sqrt(3.0 / 7.0), 0.0, math.sqrt(3.0 / 7.0), 1.0])
    quadrature = np.array([0.1, 49.0 / 90.0, 32.0 / 45.0, 49.0 / 90.0, 0.1])
    factor = np.array([np.prod([points[row_at] - points[col_at] for col_at in range(5) if col_at != row_at]) for row_at in range(5)])
    derivative = np.zeros((5, 5))
    for row_at in range(5):
        for col_at in range(5):
            if row_at != col_at:
                derivative[row_at, col_at] = factor[row_at] / (factor[col_at] * (points[row_at] - points[col_at]))
        derivative[row_at, row_at] = -np.sum(derivative[row_at])
    return (jnp.asarray(derivative, jnp.float32), jnp.asarray(quadrature, jnp.float32))

def periodic_weights(length):
    position = jnp.arange(length) % 4
    return jnp.where(position == 0, 0.2, jnp.where(position == 2, 32.0 / 45.0, 49.0 / 90.0)).astype(jnp.float32)

def lumped_mass(planes, rows_y, depth_z):
    along_z = jnp.where(jnp.arange(depth_z) == 0, 0.1, periodic_weights(depth_z)).astype(jnp.float32)
    return periodic_weights(planes)[:, None, None] * periodic_weights(rows_y)[None, :, None] * along_z[None, None, :]

def extend(field, next_plane):
    widened = jnp.concatenate([field, next_plane], 0)
    widened = jnp.concatenate([widened, widened[:, :1]], 1)
    bottom = jnp.zeros(widened.shape[:2] + (1,), widened.dtype)
    return jnp.concatenate([widened, bottom], 2)

def split_axis(field, axis_at):
    count = (field.shape[axis_at] - 1) // 4
    shape = field.shape[:axis_at] + (count, 4) + field.shape[axis_at + 1:]
    head = lax.slice_in_dim(field, 0, 4 * count, axis=axis_at).reshape(shape)
    tail = lax.slice_in_dim(field, 4, 4 * count + 1, stride=4, axis=axis_at)
    tail = jnp.expand_dims(tail, axis_at + 1)
    return jnp.concatenate([head, tail], axis_at + 1)

def to_elements(extended):
    split = split_axis(extended, 0)
    split = split_axis(split, 2)
    split = split_axis(split, 4)
    return jnp.transpose(split, (1, 3, 5, 0, 2, 4))

def merge_axis(pieces, axis_at):
    count = pieces.shape[axis_at]
    head = lax.slice_in_dim(pieces, 0, 4, axis=axis_at + 1)
    face = lax.slice_in_dim(pieces, 4, 5, axis=axis_at + 1)
    shape = pieces.shape[:axis_at] + (4 * count,) + pieces.shape[axis_at + 2:]
    zero_shape = list(face.shape)
    zero_shape[axis_at + 1] = 3
    shifted = jnp.concatenate([face, jnp.zeros(tuple(zero_shape), pieces.dtype)], axis_at + 1).reshape(shape)
    config = [(0, 0, 0)] * len(shape)
    config[axis_at] = (0, 1, 0)
    merged = lax.pad(head.reshape(shape), jnp.zeros((), pieces.dtype), config)
    config[axis_at] = (4, -3, 0)
    return merged + lax.pad(shifted, jnp.zeros((), pieces.dtype), config)

def from_elements(pieces):
    arranged = jnp.transpose(pieces, (3, 0, 4, 1, 5, 2))
    merged = merge_axis(arranged, 4)
    merged = merge_axis(merged, 2)
    return merge_axis(merged, 0)

def stiffness(elements, speed_slab, derivative, quadrature):
    highest = lax.Precision.HIGHEST
    flat = elements.reshape(5, 5, 5, -1)
    rates = speed_slab.reshape(-1)
    cube = quadrature[:, None, None] * quadrature[None, :, None] * quadrature[None, None, :]
    scaled = cube[..., None] * rates
    grad_x = jnp.einsum('lm,mbce->lbce', derivative, flat, precision=highest)
    result = jnp.einsum('la,lbce->abce', derivative, scaled * grad_x, precision=highest)
    grad_y = jnp.einsum('lm,amce->alce', derivative, flat, precision=highest)
    result = result + jnp.einsum('lb,alce->abce', derivative, scaled * grad_y, precision=highest)
    grad_z = jnp.einsum('lm,abme->able', derivative, flat, precision=highest)
    result = result + jnp.einsum('lc,able->abce', derivative, scaled * grad_z, precision=highest)
    return result.reshape(elements.shape)

def fold_y_z(forces):
    trimmed = forces[:, :, :-1]
    width_y = trimmed.shape[1] - 1
    return jnp.concatenate([trimmed[:, :1] + trimmed[:, width_y:], trimmed[:, 1:width_y]], 1)

def sample_slots(elements, elem_slab, weight_slab):
    flat = elements.reshape(125, -1)
    picked = jnp.take(flat, elem_slab, axis=1)
    return lax.optimization_barrier(jnp.sum(picked * weight_slab, 0))

def dft_tables(freqs, steps):
    angle = jnp.pi * (jnp.arange(freqs, dtype=jnp.float32) + 0.5) / freqs
    phase = angle[:, None] * jnp.arange(steps, dtype=jnp.float32)[None, :]
    return (jnp.cos(phase), -jnp.sin(phase))

def reference(wavefield_now, wavefield_vel, speed_sq, source_field, wavelet, slot_elem, slot_station, slot_weight, pair_blocks):
    derivative, quadrature = gll_tables()
    planes = 4 * EX_DEV
    mass = lumped_mass(NX, NYN, NZN)
    field_now = wavefield_now
    field_prev = wavefield_now - STEP_DT * wavefield_vel
    speed_slabs = speed_sq.reshape(DEVICES, EX_DEV, EY, EZ)
    elem_slabs = slot_elem.reshape(DEVICES, CAP)
    weight_slabs = slot_weight.reshape(125, DEVICES, CAP).transpose(1, 0, 2)

    def per_slab(inputs):
        slab_field, next_plane, speed_slab, elem_slab, weight_slab = inputs
        elements = to_elements(extend(slab_field, next_plane))
        forces = fold_y_z(from_elements(stiffness(elements, speed_slab, derivative, quadrature)))
        return (forces, sample_slots(elements, elem_slab, weight_slab))
    records = []
    for moment in range(NT):
        slabs = field_now.reshape(DEVICES, planes, NYN, NZN)
        next_planes = jnp.roll(slabs[:, :1], -1, axis=0)
        forces, samples = lax.map(per_slab, (slabs, next_planes, speed_slabs, elem_slabs, weight_slabs))
        back = jnp.roll(forces[:, planes:], 1, axis=0)
        assembled = jnp.concatenate([forces[:, :1] + back, forces[:, 1:planes]], 1).reshape(NX, NYN, NZN)
        accel = wavelet[moment] * source_field - assembled / mass
        field_next = 2.0 * field_now - field_prev + STEP_DT * STEP_DT * accel
        records.append(samples.reshape(-1))
        field_prev = field_now
        field_now = field_next
    samples_all = jnp.stack(records, 0)
    cos_table, sin_table = dft_tables(F, NT)
    highest = lax.Precision.HIGHEST
    real_part = jnp.dot(cos_table, samples_all, precision=highest, preferred_element_type=jnp.float32)
    imag_part = jnp.dot(sin_table, samples_all, precision=highest, preferred_element_type=jnp.float32)
    spectra = jnp.concatenate([real_part, imag_part], 0).astype(jnp.bfloat16)
    slot_count = DEVICES * CAP
    position = jnp.zeros((NSTA + 1,), jnp.int32).at[slot_station].set(jnp.arange(slot_count, dtype=jnp.int32))
    by_station = jnp.take(spectra, position[:NSTA], axis=1).astype(jnp.float32).reshape(2, F, NSB, SB)

    def one_pair(blocks):
        first_block = jnp.take(by_station, blocks[0], axis=2)
        second_block = jnp.take(by_station, blocks[1], axis=2)
        cross_re = (first_block[0][:, :, None] * second_block[0][:, None, :] + first_block[1][:, :, None] * second_block[1][:, None, :]) / NT
        cross_im = (first_block[1][:, :, None] * second_block[0][:, None, :] - first_block[0][:, :, None] * second_block[1][:, None, :]) / NT
        return jnp.stack([cross_re, cross_im], 0).reshape(2, F, SB * SB).astype(jnp.bfloat16)
    cross = lax.map(one_pair, pair_blocks)
    return (field_now, cross)
```

```python
import functools
import math

import jax
import jax.numpy as jnp
import numpy as np
from jax import lax
from jax.experimental import pallas as pl
from jax.experimental.pallas import tpu as pltpu
from jax.sharding import PartitionSpec as P

NT = 6
F = 256
SB = 32
STEP_DT = 0.04
MESH = pl.DeviceIdType.MESH
HIGHEST = lax.Precision.HIGHEST


def gll_tables():
    points = np.array([-1.0, -math.sqrt(3.0 / 7.0), 0.0, math.sqrt(3.0 / 7.0), 1.0])
    quadrature = np.array([0.1, 49.0 / 90.0, 32.0 / 45.0, 49.0 / 90.0, 0.1])
    factor = np.array(
        [np.prod([points[i] - points[j] for j in range(5) if j != i]) for i in range(5)]
    )
    derivative = np.zeros((5, 5))
    for i in range(5):
        for j in range(5):
            if i != j:
                derivative[i, j] = factor[i] / (factor[j] * (points[i] - points[j]))
        derivative[i, i] = -np.sum(derivative[i])
    return derivative, quadrature


DERIV, QUAD = gll_tables()
K1 = DERIV.T @ np.diag(QUAD) @ DERIV
M1 = np.array([0.2, QUAD[1], QUAD[2], QUAD[3]])
OFFSETS = (-4, -3, -2, -1, 1, 2, 3, 4, 0)


def spread_matrices(ny, nz):
    ey, ez = ny // 4, nz // 4
    wy = np.zeros((ny, ey))
    wz = np.zeros((ez, nz))
    for e in range(ey):
        for b in range(5):
            r = (4 * e + b) % ny
            wy[r, e] += QUAD[b] / M1[r % 4]
    for e in range(ez):
        for c in range(5):
            r = 4 * e + c
            if r < nz:
                wz[e, r] += QUAD[c] / (0.1 if r == 0 else M1[r % 4])
    own_y = np.zeros((ny, ey))
    prev_y = np.zeros((ny, ey))
    own_z = np.zeros((ez, nz))
    prev_z = np.zeros((ez, nz))
    for r in range(ny):
        own_y[r, r // 4] = 1
        prev_y[r, (r // 4 - 1) % ey] = 1
    for c in range(nz):
        own_z[c // 4, c] = 1
        if c >= 4:
            prev_z[c // 4 - 1, c] = 1
    left = np.concatenate([wy, own_y, prev_y], 0).astype(np.float32)
    right = np.concatenate([wz, own_z, prev_z], 1).astype(np.float32)
    return left, right


def own_factor(b, d):
    return K1[b, b + d] / M1[b] if 0 <= b + d <= 4 else 0.0


def prev_factor(b, d):
    return K1[4, 4 + d] / M1[0] if b == 0 and -4 <= d <= 0 else 0.0


def by_position(position, values):
    out = jnp.full(position.shape, values[0], jnp.float32)
    for b in range(1, 4):
        out = jnp.where(position == b, jnp.float32(values[b]), out)
    return out


def dot(a, b):
    return jnp.dot(a, b, precision=HIGHEST, preferred_element_type=jnp.float32)


def write_coefficients(speed, left, right, coef, which, cross_x):
    ny, nz = cross_x.shape
    scale = -STEP_DT * STEP_DT
    by_z = dot(speed, right[:, :nz]) * scale
    by_y = dot(left[:ny], speed) * scale
    row_own = dot(left[ny : 2 * ny], by_z)
    row_prev = dot(left[2 * ny :], by_z)
    col_own = dot(by_y, right[:, nz : 2 * nz])
    col_prev = dot(by_y, right[:, 2 * nz :])
    cross_x[...] = dot(left[:ny], by_z)
    if coef is None:
        return
    row = lax.broadcasted_iota(jnp.int32, (8, nz), 0) & 3
    lane = lax.broadcasted_iota(jnp.int32, (8, nz), 1)
    col = lane & 3
    ones = jnp.ones((ny // 8, 1, 1), jnp.float32)

    def tiled(tile):
        return (tile[None] * ones).reshape(ny, nz)

    for n, d in enumerate(OFFSETS):
        y_own = by_position(row, [own_factor(b, d) for b in range(4)])
        y_part = row_own * tiled(y_own)
        if d <= 0:
            y_part += row_prev * tiled(by_position(row, [prev_factor(b, d) for b in range(4)]))
        z_own = by_position(col, [own_factor(b, d) for b in range(4)])
        first = M1[0] / 0.1
        z_own = jnp.where(lane == 0, jnp.float32(own_factor(0, d) * first), z_own)
        z_own = jnp.where(lane + d >= nz, 0.0, z_own)
        z_part = col_own * tiled(z_own)
        if d <= 0:
            z_part += col_prev * tiled(by_position(col, [prev_factor(b, d) for b in range(4)]))
        if d == 0:
            coef[which, 16] = y_part + z_part
        else:
            coef[which, n] = y_part
            coef[which, 8 + n] = z_part


def split_two(v):
    high = v.astype(jnp.bfloat16)
    low = (v - high.astype(jnp.float32)).astype(jnp.bfloat16)
    return jnp.concatenate([high, low], 1)


def window_kernel(
    axes,
    sizes,
    now_ref,
    vel_ref,
    speed_ref,
    src_ref,
    wave_ref,
    elem_ref,
    weight_ref,
    left_ref,
    right_ref,
    end_ref,
    gath_ref,
    field,
    acc,
    coef,
    x_own,
    x_left,
    pick_z,
    pick_y,
    samp,
    send_v,
    send_p,
    recv_v,
    recv_p,
    speed_in,
    all_samp,
    ssem,
    rsem,
    speed_sem,
    all_sem,
):
    planes, ny, nz = now_ref.shape
    slots = elem_ref.shape[1]
    n = sizes[0] * sizes[1]
    me = lax.axis_index(axes[0]) * sizes[1] + lax.axis_index(axes[1])

    def device(j):
        return (j // sizes[1], j % sizes[1])

    right_dev = device((me + 1) % n)
    left_dev = device((me + n - 1) % n)

    barrier = pltpu.get_barrier_semaphore()

    @pl.loop(1, n)
    def _(off):
        pl.semaphore_signal(
            barrier, inc=1, device_id=device((me + off) % n), device_id_type=MESH
        )

    def copies(t):
        return (
            pltpu.make_async_remote_copy(
                src_ref=send_v.at[t],
                dst_ref=recv_v.at[t],
                send_sem=ssem.at[0, t],
                recv_sem=rsem.at[0, t],
                device_id=left_dev,
                device_id_type=MESH,
            ),
            pltpu.make_async_remote_copy(
                src_ref=send_p.at[t],
                dst_ref=recv_p.at[t],
                send_sem=ssem.at[1, t],
                recv_sem=rsem.at[1, t],
                device_id=right_dev,
                device_id_type=MESH,
            ),
        )

    def stage(t, u):
        send_v[t] = u[0]
        total = u[0] * jnp.float32(K1[4, 0])
        for a in range(1, 4):
            total += u[a] * jnp.float32(K1[4, a])
        send_p[t] = total

    start = [now_ref[p] for p in range(4)]
    stage(0, start)
    for p in range(4):
        field[0, p] = start[p]
        field[1, p] = start[p] - STEP_DT * vel_ref[p]

    pl.semaphore_wait(barrier, n - 1)
    speed_copy = pltpu.make_async_remote_copy(
        src_ref=speed_ref.at[0],
        dst_ref=speed_in,
        send_sem=speed_sem.at[0],
        recv_sem=speed_sem.at[1],
        device_id=right_dev,
        device_id_type=MESH,
    )
    speed_copy.start()
    for copy in copies(0):
        copy.start()

    left = left_ref[...]
    right = right_ref[...]
    own_speed = speed_ref[0]
    write_coefficients(own_speed, left, right, coef, 1, x_own)

    shift = int(math.log2(nz // 4))
    elem = elem_ref[...]
    first_y = (elem >> shift) * 4
    first_z = (elem & (nz // 4 - 1)) * 4
    z_at = lax.broadcasted_iota(jnp.int32, (nz, slots), 0)
    for c in range(5):
        hit = jnp.where(z_at == first_z + c, 1.0, 0.0).astype(jnp.bfloat16)
        pick_z[0:nz, c * slots : (c + 1) * slots] = hit
        pick_z[nz : 2 * nz, c * slots : (c + 1) * slots] = hit
    y_at = lax.broadcasted_iota(jnp.int32, (ny, slots), 0)
    rows = []
    for b in range(5):
        row = first_y + b
        rows.append(jnp.where(row >= ny, row - ny, row))
    for a in range(5):
        for c in range(5):
            value = jnp.zeros((ny, slots), jnp.float32)
            for b in range(5):
                at = 25 * a + 5 * b + c
                value = jnp.where(y_at == rows[b], weight_ref[at : at + 1, :], value)
            pick_y[a, c] = value
    samp[...] = jnp.zeros_like(samp)

    speed_copy.wait()
    left_speed = speed_in[...]
    write_coefficients(0.5 * (own_speed + left_speed), left, right, coef, 0, x_left)
    write_coefficients(left_speed, left, right, None, 0, x_left)

    def sample(a, v):
        picked = jnp.dot(split_two(v), pick_z[...], preferred_element_type=jnp.float32)
        total = picked[:, :slots] * pick_y[a, 0]
        for c in range(1, 5):
            total += picked[:, c * slots : (c + 1) * slots] * pick_y[a, c]
        return jnp.sum(total.reshape(ny // 8, 8, slots), 0)

    def partial(t, slot):
        u = [field[slot, p] for p in range(4)]
        drive = wave_ref[t] * jnp.float32(STEP_DT * STEP_DT)
        for p in range(4):
            which = 0 if p == 0 else 1
            v = field[slot, p]
            total = 2.0 * v - field[1 - slot, p] + drive * src_ref[p] + coef[which, 16] * v
            along = field[slot, 0] * jnp.float32(K1[p, 0] / M1[p])
            for a in range(1, 4):
                along += field[slot, a] * jnp.float32(K1[p, a] / M1[p])
            total += x_own[...] * along
            if p == 0:
                total += x_left[...] * (v * jnp.float32(K1[4, 4] / M1[0]))
            for i, d in enumerate(OFFSETS[:8]):
                total += coef[which, i] * pltpu.roll(v, (-d) % ny, 0)
                total += coef[which, 8 + i] * pltpu.roll(v, (-d) % nz, 1)
            acc[p] = total

    def finish(t, slot, store):
        far = recv_v[t]
        near = recv_p[t]
        shared = x_own[...] * far
        out = []
        for p in range(4):
            total = acc[p] + shared * jnp.float32(K1[p, 4] / M1[p])
            if p == 0:
                total += x_left[...] * (near * jnp.float32(1.0 / M1[0]))
            store(p, total)
            out.append(total)
        return out

    def wait_halo(t):
        for copy in copies(t):
            copy.wait_recv()

    def inner_samples(slot):
        total = sample(0, field[slot, 0])
        for a in range(1, 4):
            total += sample(a, field[slot, a])
        return total

    def step(t, carry):
        slot = t % 2
        partial(t, slot)
        taken = inner_samples(slot)
        wait_halo(t)

        def store(p, value):
            field[1 - slot, p] = value

        stage(t + 1, finish(t, slot, store))
        for copy in copies(t + 1):
            copy.start()
        taken += sample(4, recv_v[t])
        samp[pl.ds(t, 1), :] = jnp.sum(taken, 0, keepdims=True)
        return carry

    lax.fori_loop(0, NT - 1, step, 0)

    last = NT - 1
    slot = last % 2
    partial(last, slot)
    taken = inner_samples(slot)
    wait_halo(last)
    taken += sample(4, recv_v[last])
    samp[last : last + 1, :] = jnp.sum(taken, 0, keepdims=True)

    @pl.loop(1, n)
    def _(off):
        pltpu.make_async_remote_copy(
            src_ref=samp,
            dst_ref=all_samp.at[me],
            send_sem=all_sem.at[0],
            recv_sem=all_sem.at[1],
            device_id=device((me + off) % n),
            device_id_type=MESH,
        ).start()

    def store_end(p, value):
        end_ref[p] = value

    finish(last, slot, store_end)
    whole = all_samp.at[pl.ds(0, n - 1)]
    everyone = pltpu.make_async_remote_copy(
        src_ref=whole,
        dst_ref=whole,
        send_sem=all_sem.at[0],
        recv_sem=all_sem.at[1],
        device_id=right_dev,
        device_id_type=MESH,
    )
    everyone.wait_recv()
    all_samp[me] = samp[...]
    gath_ref[...] = all_samp[...]
    everyone.wait_send()

    def drain(t, carry):
        for copy in copies(t):
            copy.wait_send()
        return carry

    lax.fori_loop(0, NT, drain, 0)


def split_three(v):
    high = v.astype(jnp.bfloat16).astype(jnp.float32)
    rest = v - high
    middle = rest.astype(jnp.bfloat16).astype(jnp.float32)
    return high, middle, rest - middle


def cross_kernel(gath_ref, station_ref, blocks_ref, table_ref, out_ref, waves):
    n, _, slots = gath_ref.shape
    lanes = SB * SB
    pair = pl.program_id(0)

    @pl.when(pl.program_id(1) == 0)
    def _():
        first = blocks_ref[pair, 0]
        second = blocks_ref[pair, 1]
        k = lax.broadcasted_iota(jnp.int32, (2 * SB, slots), 0)
        wanted = jnp.where(k < SB, first * SB + k, second * SB + k - SB)
        hits = []
        parts = []
        for d in range(n):
            hit = wanted == station_ref[d : d + 1, :]
            hits.append(jnp.where(hit, 1.0, 0.0).astype(jnp.bfloat16))
            high, middle, low = split_three(gath_ref[d])
            parts.append(jnp.concatenate([high, middle, low, jnp.zeros_like(low)], 0))
        picked = lax.dot_general(
            jnp.concatenate(parts, 1).astype(jnp.bfloat16),
            jnp.concatenate(hits, 1),
            (((1,), (1,)), ((), ())),
            preferred_element_type=jnp.float32,
        )
        row = lax.broadcasted_iota(jnp.int32, (2 * SB, 2 * lanes), 0)
        lane = lax.broadcasted_iota(jnp.int32, (2 * SB, 2 * lanes), 1)
        source = jnp.where(lane < lanes, lane // SB, SB + lane % SB)
        spread = jnp.where(row == source, 1.0, 0.0).astype(jnp.bfloat16)
        wide = jnp.dot(
            picked.astype(jnp.bfloat16), spread, preferred_element_type=jnp.float32
        )
        high, middle, low = wide[0:8], wide[8:16], wide[16:24]
        waves[...] = jnp.concatenate([high, middle, high, low, high, middle], 0).astype(
            jnp.bfloat16
        )

    def spectrum(part):
        full = jnp.dot(table_ref[part], waves[...], preferred_element_type=jnp.float32)
        full = full.astype(jnp.bfloat16).astype(jnp.float32)
        return full[:, :lanes], full[:, lanes:]

    re_a, re_b = spectrum(0)
    im_a, im_b = spectrum(1)
    out_ref[0, 0] = ((re_a * re_b + im_a * im_b) * jnp.float32(1.0 / NT)).astype(jnp.bfloat16)
    out_ref[0, 1] = ((im_a * re_b - re_a * im_b) * jnp.float32(1.0 / NT)).astype(jnp.bfloat16)


def dft_table():
    angle = np.pi * (np.arange(F) + 0.5) / F
    phase = angle[:, None] * np.arange(8)[None, :]
    live = np.arange(8) < NT
    parts = []
    for table in (np.cos(phase) * live, -np.sin(phase) * live):
        table = table.astype(np.float32)
        high = table.astype(jnp.bfloat16).astype(np.float32)
        middle = (table - high).astype(jnp.bfloat16).astype(np.float32)
        low = table - high - middle
        parts.append(np.concatenate([high, high, middle, high, low, middle], 1))
    return jnp.asarray(np.stack(parts).astype(jnp.bfloat16))


def vmem(count):
    return [pl.BlockSpec(memory_space=pltpu.VMEM)] * count


def body(axes, sizes, *args):
    now, vel, speed, source, wavelet, elem, station, weight, blocks = args
    planes, ny, nz = now.shape
    slots = elem.shape[0]
    n = sizes[0] * sizes[1]
    left, right = spread_matrices(ny, nz)
    f32, bf16 = jnp.float32, jnp.bfloat16
    end, gath = pl.pallas_call(
        functools.partial(window_kernel, axes, sizes),
        out_shape=(
            jax.ShapeDtypeStruct(now.shape, f32),
            jax.ShapeDtypeStruct((n, 8, slots), f32),
        ),
        in_specs=vmem(4) + [pl.BlockSpec(memory_space=pltpu.SMEM)] + vmem(4),
        out_specs=tuple(vmem(2)),
        scratch_shapes=[
            pltpu.VMEM((2, planes, ny, nz), f32),
            pltpu.VMEM((planes, ny, nz), f32),
            pltpu.VMEM((2, 17, ny, nz), f32),
            pltpu.VMEM((ny, nz), f32),
            pltpu.VMEM((ny, nz), f32),
            pltpu.VMEM((2 * nz, 5 * slots), bf16),
            pltpu.VMEM((5, 5, ny, slots), f32),
            pltpu.VMEM((8, slots), f32),
            pltpu.VMEM((NT, ny, nz), f32),
            pltpu.VMEM((NT, ny, nz), f32),
            pltpu.VMEM((NT, ny, nz), f32),
            pltpu.VMEM((NT, ny, nz), f32),
            pltpu.VMEM((ny // 4, nz // 4), f32),
            pltpu.VMEM((n, 8, slots), f32),
            pltpu.SemaphoreType.DMA((2, NT)),
            pltpu.SemaphoreType.DMA((2, NT)),
            pltpu.SemaphoreType.DMA((2,)),
            pltpu.SemaphoreType.DMA((2,)),
        ],
        compiler_params=pltpu.CompilerParams(
            collective_id=0, has_side_effects=True, vmem_limit_bytes=32 * 2**20
        ),
        name="window",
    )(
        now,
        vel,
        speed,
        source,
        wavelet,
        elem.reshape(1, slots),
        weight,
        jnp.asarray(left),
        jnp.asarray(right),
    )
    pairs = blocks.shape[0]
    chunk = 64
    cross = pl.pallas_call(
        cross_kernel,
        out_shape=jax.ShapeDtypeStruct((pairs, 2, F, SB * SB), bf16),
        grid=(pairs, F // chunk),
        in_specs=[
            pl.BlockSpec((n, 8, slots), lambda p, f: (0, 0, 0)),
            pl.BlockSpec((n, slots), lambda p, f: (0, 0)),
            pl.BlockSpec(memory_space=pltpu.SMEM),
            pl.BlockSpec((2, chunk, 48), lambda p, f: (0, f, 0)),
        ],
        out_specs=pl.BlockSpec((1, 2, chunk, SB * SB), lambda p, f: (p, 0, f, 0)),
        scratch_shapes=[pltpu.VMEM((48, 2 * SB * SB), bf16)],
        compiler_params=pltpu.CompilerParams(vmem_limit_bytes=32 * 2**20),
        name="cross",
    )(gath, station.reshape(n, slots), blocks, dft_table())
    return end, cross


def solution(mesh):
    axes = ("pair", "bulk")
    sizes = tuple(mesh.shape[a] for a in axes)
    split = P(axes, None, None)
    in_specs = (
        split,
        split,
        split,
        split,
        P(),
        P(axes),
        P(),
        P(None, axes),
        P(axes, None),
    )
    return jax.shard_map(
        functools.partial(body, axes, sizes),
        mesh=mesh,
        in_specs=in_specs,
        out_specs=(split, P(axes, None, None, None)),
        check_vma=False,
    )
```

```python
import functools
import math

import jax
import jax.numpy as jnp
import numpy as np
from jax import lax
from jax.experimental import pallas as pl
from jax.experimental.pallas import tpu as pltpu
from jax.sharding import PartitionSpec as P

NT = 6
F = 256
SB = 32
STEP_DT = 0.04
MESH = pl.DeviceIdType.MESH
HIGHEST = lax.Precision.HIGHEST


def gll_tables():
    points = np.array([-1.0, -math.sqrt(3.0 / 7.0), 0.0, math.sqrt(3.0 / 7.0), 1.0])
    quadrature = np.array([0.1, 49.0 / 90.0, 32.0 / 45.0, 49.0 / 90.0, 0.1])
    factor = np.array(
        [np.prod([points[i] - points[j] for j in range(5) if j != i]) for i in range(5)]
    )
    derivative = np.zeros((5, 5))
    for i in range(5):
        for j in range(5):
            if i != j:
                derivative[i, j] = factor[i] / (factor[j] * (points[i] - points[j]))
        derivative[i, i] = -np.sum(derivative[i])
    return derivative, quadrature


DERIV, QUAD = gll_tables()
K1 = DERIV.T @ np.diag(QUAD) @ DERIV
M1 = np.array([0.2, QUAD[1], QUAD[2], QUAD[3]])
OFFSETS = (-4, -3, -2, -1, 1, 2, 3, 4, 0)


def spread_matrices(ny, nz):
    ey, ez = ny // 4, nz // 4
    wy = np.zeros((ny, ey))
    wz = np.zeros((ez, nz))
    for e in range(ey):
        for b in range(5):
            r = (4 * e + b) % ny
            wy[r, e] += QUAD[b] / M1[r % 4]
    for e in range(ez):
        for c in range(5):
            r = 4 * e + c
            if r < nz:
                wz[e, r] += QUAD[c] / (0.1 if r == 0 else M1[r % 4])
    own_y = np.zeros((ny, ey))
    prev_y = np.zeros((ny, ey))
    own_z = np.zeros((ez, nz))
    prev_z = np.zeros((ez, nz))
    for r in range(ny):
        own_y[r, r // 4] = 1
        prev_y[r, (r // 4 - 1) % ey] = 1
    for c in range(nz):
        own_z[c // 4, c] = 1
        if c >= 4:
            prev_z[c // 4 - 1, c] = 1
    left = np.concatenate([wy, own_y, prev_y], 0).astype(np.float32)
    right = np.concatenate([wz, own_z, prev_z], 1).astype(np.float32)
    return left, right


def own_factor(b, d):
    return K1[b, b + d] / M1[b] if 0 <= b + d <= 4 else 0.0


def prev_factor(b, d):
    return K1[4, 4 + d] / M1[0] if b == 0 and -4 <= d <= 0 else 0.0


def by_position(position, values):
    out = jnp.full(position.shape, values[0], jnp.float32)
    for b in range(1, 4):
        out = jnp.where(position == b, jnp.float32(values[b]), out)
    return out


def dot(a, b):
    return jnp.dot(a, b, precision=HIGHEST, preferred_element_type=jnp.float32)


def speed_parts(speed, left, right):
    ny, nz = left.shape[0] // 3, right.shape[1] // 3
    scale = -STEP_DT * STEP_DT
    rows = dot(left, dot(speed, right[:, :nz]) * scale)
    cols = dot(dot(left[:ny], speed) * scale, right[:, nz:])
    return rows[:ny], rows[ny : 2 * ny], rows[2 * ny :], cols[:, :nz], cols[:, nz:]


def write_coefficients(parts, coef, which):
    row_own, row_prev, col_own, col_prev = parts
    ny, nz = row_own.shape
    row = lax.broadcasted_iota(jnp.int32, (8, nz), 0) & 3
    lane = lax.broadcasted_iota(jnp.int32, (8, nz), 1)
    col = lane & 3

    def times(values, tile):
        return (values.reshape(ny // 8, 8, nz) * tile[None]).reshape(ny, nz)

    for i, d in enumerate(OFFSETS):
        y_part = times(row_own, by_position(row, [own_factor(b, d) for b in range(4)]))
        if d <= 0:
            y_part += times(row_prev, by_position(row, [prev_factor(b, d) for b in range(4)]))
        z_own = by_position(col, [own_factor(b, d) for b in range(4)])
        z_own = jnp.where(lane == 0, jnp.float32(own_factor(0, d) * M1[0] / 0.1), z_own)
        z_own = jnp.where(lane + d >= nz, 0.0, z_own)
        z_part = times(col_own, z_own)
        if d <= 0:
            z_part += times(col_prev, by_position(col, [prev_factor(b, d) for b in range(4)]))
        if d == 0:
            coef[which, 16] = y_part + z_part
        else:
            coef[which, i] = y_part
            coef[which, 8 + i] = z_part


def split_two(v):
    high = v.astype(jnp.bfloat16)
    low = (v - high.astype(jnp.float32)).astype(jnp.bfloat16)
    return jnp.concatenate([high, low], 1)


def write_pick_z(elem, pick_z):
    slots = elem.shape[1]
    nz = pick_z.shape[0] // 2
    first_z = (elem & (nz // 4 - 1)) * 4
    z_at = lax.broadcasted_iota(jnp.int32, (nz, slots), 0)
    for c in range(5):
        hit = jnp.where(z_at == first_z + c, 1.0, 0.0).astype(jnp.bfloat16)
        pick_z[0:nz, c * slots : (c + 1) * slots] = hit
        pick_z[nz : 2 * nz, c * slots : (c + 1) * slots] = hit


def write_pick_y(elem, weight, layers, pick_y, nz):
    slots = elem.shape[1]
    ny = pick_y.shape[1] // len(layers)
    first_y = (elem >> int(math.log2(nz // 4))) * 4
    y_at = lax.broadcasted_iota(jnp.int32, (ny, slots), 0)
    rows = []
    for b in range(5):
        row = first_y + b
        rows.append(jnp.where(row >= ny, row - ny, row))
    for i, a in enumerate(layers):
        for c in range(5):
            value = jnp.zeros((ny, slots), jnp.float32)
            for b in range(5):
                value = jnp.where(y_at == rows[b], weight(a, b, c), value)
            pick_y[c, i * ny : (i + 1) * ny] = value


def sample(values, pick_z, pick_y):
    rows = values.shape[0]
    slots = pick_y.shape[2]
    total = jnp.zeros((rows, slots), jnp.float32)
    for c in (0, 2, 4):
        some = min(2, 5 - c)
        picked = jnp.dot(
            values,
            pick_z[:, c * slots : (c + some) * slots],
            preferred_element_type=jnp.float32,
        )
        for k in range(some):
            total += picked[:, k * slots : (k + 1) * slots] * pick_y[c + k]
    return jnp.sum(jnp.sum(total.reshape(rows // 8, 8, slots), 0), 0, keepdims=True)


def split_three(v):
    high = v.astype(jnp.bfloat16).astype(jnp.float32)
    rest = v - high
    middle = rest.astype(jnp.bfloat16).astype(jnp.float32)
    return high, middle, rest - middle


def window_kernel(
    axes,
    sizes,
    now_hbm,
    vel_hbm,
    speed_hbm,
    src_hbm,
    elem_hbm,
    weight_hbm,
    left_hbm,
    right_hbm,
    station_hbm,
    wave_ref,
    blocks_ref,
    end_ref,
    picked_ref,
    now_ref,
    vel_ref,
    speed_ref,
    src_ref,
    elem_ref,
    weight_ref,
    left_ref,
    right_ref,
    station_ref,
    field,
    acc,
    coef,
    x_own,
    x_left,
    pick_z,
    pick_y,
    pick_z_left,
    pick_y_left,
    hits,
    samp,
    setup_out,
    setup_in,
    send_v,
    send_p,
    recv_v,
    recv_p,
    all_samp,
    load_sem,
    ssem,
    rsem,
    setup_sem,
    all_sem,
):
    planes, ny, nz = now_ref.shape
    slots = elem_ref.shape[1]
    n = sizes[0] * sizes[1]
    me = lax.axis_index(axes[0]) * sizes[1] + lax.axis_index(axes[1])

    loads = [
        pltpu.make_async_copy(src, dst, load_sem.at[i])
        for i, (src, dst) in enumerate(
            [
                (now_hbm, now_ref),
                (speed_hbm, speed_ref),
                (elem_hbm, elem_ref),
                (weight_hbm, weight_ref),
                (left_hbm, left_ref),
                (right_hbm, right_ref),
                (vel_hbm, vel_ref),
                (src_hbm, src_ref),
                (station_hbm, station_ref),
            ]
        )
    ]
    for load in loads:
        load.start()

    def device(j):
        return (j // sizes[1], j % sizes[1])

    right_dev = device((me + 1) % n)
    left_dev = device((me + n - 1) % n)

    barrier = pltpu.get_barrier_semaphore()

    @pl.loop(1, n)
    def _(off):
        pl.semaphore_signal(
            barrier, inc=1, device_id=device((me + off) % n), device_id_type=MESH
        )

    def copies(t):
        return (
            pltpu.make_async_remote_copy(
                src_ref=send_v.at[t],
                dst_ref=recv_v.at[t],
                send_sem=ssem.at[0, t],
                recv_sem=rsem.at[0, t],
                device_id=left_dev,
                device_id_type=MESH,
            ),
            pltpu.make_async_remote_copy(
                src_ref=send_p.at[t],
                dst_ref=recv_p.at[t],
                send_sem=ssem.at[1, t],
                recv_sem=rsem.at[1, t],
                device_id=right_dev,
                device_id_type=MESH,
            ),
        )

    def stage(t, u):
        send_v[t] = u[0].astype(jnp.bfloat16)
        total = u[0] * jnp.float32(K1[4, 0])
        for a in range(1, 4):
            total += u[a] * jnp.float32(K1[4, a])
        send_p[t] = total.astype(jnp.bfloat16)

    setup = pltpu.make_async_remote_copy(
        src_ref=setup_out,
        dst_ref=setup_in,
        send_sem=setup_sem.at[0],
        recv_sem=setup_sem.at[1],
        device_id=right_dev,
        device_id_type=MESH,
    )
    ey, ez = ny // 4, nz // 4
    setup_out[...] = jnp.zeros_like(setup_out)
    for load in loads[:4]:
        load.wait()
    elem = elem_ref[...]
    own_speed = speed_ref[0]
    setup_out[0:25] = weight_ref[100:125]
    setup_out[25:26] = elem.astype(jnp.float32)
    setup_out[32 : 32 + ey, 0:ez] = own_speed
    stage(0, [now_ref[p] for p in range(4)])

    pl.semaphore_wait(barrier, n - 1)
    setup.start()
    for copy in copies(0):
        copy.start()

    for load in loads[4:]:
        load.wait()
    for p in range(4):
        value = now_ref[p]
        field[0, p] = value
        field[1, p] = value - STEP_DT * vel_ref[p]
    left = left_ref[...]
    right = right_ref[...]
    own = speed_parts(own_speed, left, right)
    x_own[...] = own[0]
    write_coefficients(own[1:], coef, 1)
    write_pick_z(elem, pick_z)
    write_pick_y(
        elem,
        lambda a, b, c: weight_ref[25 * a + 5 * b + c : 25 * a + 5 * b + c + 1, :],
        range(4),
        pick_y,
        nz,
    )
    samp[...] = jnp.zeros_like(samp)

    setup.wait()
    before = speed_parts(setup_in[32 : 32 + ey, 0:ez], left, right)
    x_left[...] = before[0]
    write_coefficients([0.5 * (i + j) for i, j in zip(own[1:], before[1:])], coef, 0)

    def partial(t, slot):
        drive = wave_ref[t] * jnp.float32(STEP_DT * STEP_DT)
        for p in range(4):
            which = 0 if p == 0 else 1
            v = field[slot, p]
            total = 2.0 * v - field[1 - slot, p] + drive * src_ref[p] + coef[which, 16] * v
            along = field[slot, 0] * jnp.float32(K1[p, 0] / M1[p])
            for a in range(1, 4):
                along += field[slot, a] * jnp.float32(K1[p, a] / M1[p])
            total += x_own[...] * along
            if p == 0:
                total += x_left[...] * (v * jnp.float32(K1[4, 4] / M1[0]))
            for i, d in enumerate(OFFSETS[:8]):
                total += coef[which, i] * pltpu.roll(v, (-d) % ny, 0)
                total += coef[which, 8 + i] * pltpu.roll(v, (-d) % nz, 1)
            acc[p] = total

    def finish(t, store):
        for copy in copies(t):
            copy.wait_recv()
        shared = x_own[...] * recv_v[t].astype(jnp.float32)
        out = []
        for p in range(4):
            total = acc[p] + shared * jnp.float32(K1[p, 4] / M1[p])
            if p == 0:
                near = recv_p[t].astype(jnp.float32)
                total += x_left[...] * (near * jnp.float32(1.0 / M1[0]))
            store(p, total)
            out.append(total)
        return out

    def take_samples(t, slot):
        values = jnp.concatenate([split_two(field[slot, p]) for p in range(4)], 0)
        samp[pl.ds(t, 1), :] = sample(values, pick_z, pick_y)
        samp[pl.ds(t + 8, 1), :] = sample(values[:ny], pick_z_left, pick_y_left)

    def advance(t, slot):
        def store(p, value):
            field[1 - slot, p] = value

        stage(t + 1, finish(t, store))
        for copy in copies(t + 1):
            copy.start()

    partial(0, 0)
    advance(0, 0)

    left_elem = setup_in[25:26].astype(jnp.int32)
    write_pick_z(left_elem, pick_z_left)
    write_pick_y(
        left_elem,
        lambda a, b, c: setup_in[5 * b + c : 5 * b + c + 1, :],
        range(4, 5),
        pick_y_left,
        nz,
    )
    take_samples(0, 0)
    for pair in range(hits.shape[0] // (2 * SB)):
        first = blocks_ref[pair, 0]
        second = blocks_ref[pair, 1]
        k = lax.broadcasted_iota(jnp.int32, (2 * SB, slots), 0)
        wanted = jnp.where(k < SB, first * SB + k, second * SB + k - SB)
        for d in range(n):
            hit = jnp.where(wanted == station_ref[d : d + 1, :], 1.0, 0.0)
            hits[pair * 2 * SB : (pair + 1) * 2 * SB, d * slots : (d + 1) * slots] = hit.astype(
                jnp.bfloat16
            )

    def step(t, carry):
        slot = t % 2
        partial(t, slot)
        take_samples(t, slot)
        advance(t, slot)
        return carry

    lax.fori_loop(1, NT - 1, step, 0)

    last = NT - 1
    slot = last % 2
    take_samples(last, slot)

    @pl.loop(1, n)
    def _(off):
        pltpu.make_async_remote_copy(
            src_ref=samp,
            dst_ref=all_samp.at[me],
            send_sem=all_sem.at[0],
            recv_sem=all_sem.at[1],
            device_id=device((me + off) % n),
            device_id_type=MESH,
        ).start()

    partial(last, slot)

    def store_end(p, value):
        end_ref[p] = value

    finish(last, store_end)
    whole = all_samp.at[pl.ds(0, n - 1)]
    everyone = pltpu.make_async_remote_copy(
        src_ref=whole,
        dst_ref=whole,
        send_sem=all_sem.at[0],
        recv_sem=all_sem.at[1],
        device_id=right_dev,
        device_id_type=MESH,
    )
    everyone.wait_recv()
    all_samp[me] = samp[...]
    parts = []
    for d in range(n):
        high, middle, low = split_three(all_samp[d, 0:8] + all_samp[(d + 1) % n, 8:16])
        parts.append(jnp.concatenate([high, middle, low, jnp.zeros_like(low)], 0))
    picked_ref[...] = lax.dot_general(
        jnp.concatenate(parts, 1).astype(jnp.bfloat16),
        hits[...],
        (((1,), (1,)), ((), ())),
        preferred_element_type=jnp.float32,
    )
    everyone.wait_send()

    def drain(t, carry):
        for copy in copies(t):
            copy.wait_send()
        return carry

    lax.fori_loop(0, NT, drain, 0)


def cross_kernel(picked_ref, end_ref, table_ref, out_ref, final_ref, waves, sem):
    lanes = SB * SB
    pair = pl.program_id(0)
    chunk = pl.program_id(1)
    carry = pltpu.make_async_copy(end_ref, final_ref, sem)

    @pl.when((pair == 0) & (chunk == 0))
    def _():
        carry.start()

    @pl.when(chunk == 0)
    def _():
        row = lax.broadcasted_iota(jnp.int32, (2 * SB, 2 * lanes), 0)
        lane = lax.broadcasted_iota(jnp.int32, (2 * SB, 2 * lanes), 1)
        source = jnp.where(lane < lanes, lane // SB, SB + lane % SB)
        spread = jnp.where(row == source, 1.0, 0.0).astype(jnp.bfloat16)
        wide = jnp.dot(
            picked_ref[0].astype(jnp.bfloat16), spread, preferred_element_type=jnp.float32
        )
        high, middle, low = wide[0:8], wide[8:16], wide[16:24]
        waves[...] = jnp.concatenate([high, middle, high, low, high, middle], 0).astype(
            jnp.bfloat16
        )

    def spectrum(part):
        full = jnp.dot(table_ref[part], waves[...], preferred_element_type=jnp.float32)
        full = full.astype(jnp.bfloat16).astype(jnp.float32)
        return full[:, :lanes], full[:, lanes:]

    re_a, re_b = spectrum(0)
    im_a, im_b = spectrum(1)
    out_ref[0, 0] = ((re_a * re_b + im_a * im_b) * jnp.float32(1.0 / NT)).astype(jnp.bfloat16)
    out_ref[0, 1] = ((im_a * re_b - re_a * im_b) * jnp.float32(1.0 / NT)).astype(jnp.bfloat16)

    @pl.when((pair == pl.num_programs(0) - 1) & (chunk == pl.num_programs(1) - 1))
    def _():
        carry.wait()


def dft_table():
    angle = np.pi * (np.arange(F) + 0.5) / F
    phase = angle[:, None] * np.arange(8)[None, :]
    live = np.arange(8) < NT
    parts = []
    for table in (np.cos(phase) * live, -np.sin(phase) * live):
        table = table.astype(np.float32)
        high = table.astype(jnp.bfloat16).astype(np.float32)
        middle = (table - high).astype(jnp.bfloat16).astype(np.float32)
        low = table - high - middle
        parts.append(np.concatenate([high, high, middle, high, low, middle], 1))
    return jnp.asarray(np.stack(parts).astype(jnp.bfloat16))


def body(axes, sizes, *args):
    now, vel, speed, source, wavelet, elem, station, weight, blocks = args
    planes, ny, nz = now.shape
    slots = elem.shape[0]
    n = sizes[0] * sizes[1]
    pairs = blocks.shape[0]
    left, right = spread_matrices(ny, nz)
    f32, bf16 = jnp.float32, jnp.bfloat16
    anywhere = pl.BlockSpec(memory_space=pl.ANY)
    operands = (
        now,
        vel,
        speed,
        source,
        elem.reshape(1, slots),
        weight,
        jnp.asarray(left),
        jnp.asarray(right),
        station.reshape(n, slots),
    )
    end, picked = pl.pallas_call(
        functools.partial(window_kernel, axes, sizes),
        out_shape=(
            jax.ShapeDtypeStruct(now.shape, f32),
            jax.ShapeDtypeStruct((32, pairs * 2 * SB), f32),
        ),
        in_specs=[anywhere] * len(operands) + [pl.BlockSpec(memory_space=pltpu.SMEM)] * 2,
        out_specs=tuple([pl.BlockSpec(memory_space=pltpu.VMEM)] * 2),
        scratch_shapes=[pltpu.VMEM(x.shape, x.dtype) for x in operands]
        + [
            pltpu.VMEM((2, planes, ny, nz), f32),
            pltpu.VMEM((planes, ny, nz), f32),
            pltpu.VMEM((2, 17, ny, nz), f32),
            pltpu.VMEM((ny, nz), f32),
            pltpu.VMEM((ny, nz), f32),
            pltpu.VMEM((2 * nz, 5 * slots), bf16),
            pltpu.VMEM((5, planes * ny, slots), f32),
            pltpu.VMEM((2 * nz, 5 * slots), bf16),
            pltpu.VMEM((5, ny, slots), f32),
            pltpu.VMEM((pairs * 2 * SB, n * slots), bf16),
            pltpu.VMEM((16, slots), f32),
            pltpu.VMEM((32 + ny // 4, slots), f32),
            pltpu.VMEM((32 + ny // 4, slots), f32),
            pltpu.VMEM((NT, ny, nz), bf16),
            pltpu.VMEM((NT, ny, nz), bf16),
            pltpu.VMEM((NT, ny, nz), bf16),
            pltpu.VMEM((NT, ny, nz), bf16),
            pltpu.VMEM((n, 16, slots), f32),
            pltpu.SemaphoreType.DMA((len(operands),)),
            pltpu.SemaphoreType.DMA((2, NT)),
            pltpu.SemaphoreType.DMA((2, NT)),
            pltpu.SemaphoreType.DMA((2,)),
            pltpu.SemaphoreType.DMA((2,)),
        ],
        compiler_params=pltpu.CompilerParams(
            collective_id=0, has_side_effects=True, vmem_limit_bytes=56 * 2**20
        ),
        name="window",
    )(*operands, wavelet, blocks)
    chunk = F // 2
    cross, final = pl.pallas_call(
        cross_kernel,
        out_shape=(
            jax.ShapeDtypeStruct((pairs, 2, F, SB * SB), bf16),
            jax.ShapeDtypeStruct(now.shape, f32),
        ),
        grid=(pairs, F // chunk),
        in_specs=[
            pl.BlockSpec((1, 32, 2 * SB), lambda p, f: (p, 0, 0)),
            anywhere,
            pl.BlockSpec((2, chunk, 48), lambda p, f: (0, f, 0)),
        ],
        out_specs=(
            pl.BlockSpec((1, 2, chunk, SB * SB), lambda p, f: (p, 0, f, 0)),
            anywhere,
        ),
        scratch_shapes=[pltpu.VMEM((48, 2 * SB * SB), bf16), pltpu.SemaphoreType.DMA(())],
        compiler_params=pltpu.CompilerParams(vmem_limit_bytes=32 * 2**20),
        name="cross",
    )(picked.reshape(32, pairs, 2 * SB).transpose(1, 0, 2), end, dft_table())
    return final, cross


def solution(mesh):
    axes = ("pair", "bulk")
    sizes = tuple(mesh.shape[a] for a in axes)
    split = P(axes, None, None)
    in_specs = (
        split,
        split,
        split,
        split,
        P(),
        P(axes),
        P(),
        P(None, axes),
        P(axes, None),
    )
    return jax.shard_map(
        functools.partial(body, axes, sizes),
        mesh=mesh,
        in_specs=in_specs,
        out_specs=(split, P(axes, None, None, None)),
        check_vma=False,
    )
```

```python
import functools
import math

import jax
import jax.numpy as jnp
import numpy as np
from jax import lax
from jax.experimental import pallas as pl
from jax.experimental.pallas import tpu as pltpu
from jax.sharding import PartitionSpec as P

NT = 6
F = 256
SB = 32
STEP_DT = 0.04
MESH = pl.DeviceIdType.MESH


def gll_tables():
    points = np.array([-1.0, -math.sqrt(3.0 / 7.0), 0.0, math.sqrt(3.0 / 7.0), 1.0])
    quadrature = np.array([0.1, 49.0 / 90.0, 32.0 / 45.0, 49.0 / 90.0, 0.1])
    factor = np.array(
        [np.prod([points[i] - points[j] for j in range(5) if j != i]) for i in range(5)]
    )
    derivative = np.zeros((5, 5))
    for i in range(5):
        for j in range(5):
            if i != j:
                derivative[i, j] = factor[i] / (factor[j] * (points[i] - points[j]))
        derivative[i, i] = -np.sum(derivative[i])
    return derivative, quadrature


DERIV, QUAD = gll_tables()
K1 = DERIV.T @ np.diag(QUAD) @ DERIV
M1 = np.array([0.2, QUAD[1], QUAD[2], QUAD[3]])
OFFSETS = (-4, -3, -2, -1, 1, 2, 3, 4, 0)


def spread_matrices(ny, nz):
    ey, ez = ny // 4, nz // 4
    wy = np.zeros((ny, ey))
    wz = np.zeros((ez, nz))
    for e in range(ey):
        for b in range(5):
            r = (4 * e + b) % ny
            wy[r, e] += QUAD[b] / M1[r % 4]
    for e in range(ez):
        for c in range(5):
            r = 4 * e + c
            if r < nz:
                wz[e, r] += QUAD[c] / (0.1 if r == 0 else M1[r % 4])
    own_y = np.zeros((ny, ey))
    prev_y = np.zeros((ny, ey))
    own_z = np.zeros((ez, nz))
    prev_z = np.zeros((ez, nz))
    for r in range(ny):
        own_y[r, r // 4] = 1
        prev_y[r, (r // 4 - 1) % ey] = 1
    for c in range(nz):
        own_z[c // 4, c] = 1
        if c >= 4:
            prev_z[c // 4 - 1, c] = 1
    left = np.concatenate([wy, own_y, prev_y], 0).astype(np.float32)
    right = np.concatenate([wz, own_z, prev_z], 1).astype(np.float32)
    return left, right


def own_factor(b, d):
    return K1[b, b + d] / M1[b] if 0 <= b + d <= 4 else 0.0


def prev_factor(b, d):
    return K1[4, 4 + d] / M1[0] if b == 0 and -4 <= d <= 0 else 0.0


def by_position(position, values):
    out = jnp.full(position.shape, values[0], jnp.float32)
    for b in range(1, 4):
        out = jnp.where(position == b, jnp.float32(values[b]), out)
    return out


def high_low(v):
    high = v.astype(jnp.bfloat16).astype(jnp.float32)
    return high, v - high


def spread_right(v, constant):
    both = jnp.concatenate(high_low(v), 1).astype(jnp.bfloat16)
    twice = jnp.concatenate([constant, constant], 0).astype(jnp.bfloat16)
    return jnp.dot(both, twice, preferred_element_type=jnp.float32)


def spread_left(constant, v):
    both = jnp.concatenate(high_low(v), 0).astype(jnp.bfloat16)
    twice = jnp.concatenate([constant, constant], 1).astype(jnp.bfloat16)
    return jnp.dot(twice, both, preferred_element_type=jnp.float32)


def speed_parts(speed, left, right):
    ny, nz = left.shape[0] // 3, right.shape[1] // 3
    scale = -STEP_DT * STEP_DT
    rows = spread_left(left, spread_right(speed, right[:, :nz]) * scale)
    cols = spread_right(spread_left(left[:ny], speed) * scale, right[:, nz:])
    return rows[:ny], rows[ny : 2 * ny], rows[2 * ny :], cols[:, :nz], cols[:, nz:]


def write_coefficients(parts, coef, which):
    row_own, row_prev, col_own, col_prev = parts
    ny, nz = row_own.shape
    row = lax.broadcasted_iota(jnp.int32, (8, nz), 0) & 3
    lane = lax.broadcasted_iota(jnp.int32, (8, nz), 1)
    col = lane & 3

    def times(values, tile):
        return (values.reshape(ny // 8, 8, nz) * tile[None]).reshape(ny, nz)

    for i, d in enumerate(OFFSETS):
        y_part = times(row_own, by_position(row, [own_factor(b, d) for b in range(4)]))
        if d <= 0:
            y_part += times(row_prev, by_position(row, [prev_factor(b, d) for b in range(4)]))
        z_own = by_position(col, [own_factor(b, d) for b in range(4)])
        z_own = jnp.where(lane == 0, jnp.float32(own_factor(0, d) * M1[0] / 0.1), z_own)
        z_own = jnp.where(lane + d >= nz, 0.0, z_own)
        z_part = times(col_own, z_own)
        if d <= 0:
            z_part += times(col_prev, by_position(col, [prev_factor(b, d) for b in range(4)]))
        if d == 0:
            coef[which, 16] = y_part + z_part
        else:
            coef[which, i] = y_part
            coef[which, 8 + i] = z_part


def split_two(v):
    high = v.astype(jnp.bfloat16)
    low = (v - high.astype(jnp.float32)).astype(jnp.bfloat16)
    return jnp.concatenate([high, low], 1)


def write_pick_z(elem, pick_z):
    slots = elem.shape[1]
    nz = pick_z.shape[0] // 2
    first_z = (elem & (nz // 4 - 1)) * 4
    z_at = lax.broadcasted_iota(jnp.int32, (nz, slots), 0)
    for c in range(5):
        hit = jnp.where(z_at == first_z + c, 1.0, 0.0).astype(jnp.bfloat16)
        pick_z[0:nz, c * slots : (c + 1) * slots] = hit
        pick_z[nz : 2 * nz, c * slots : (c + 1) * slots] = hit


def write_pick_y(elem, weight, layers, pick_y, nz):
    slots = elem.shape[1]
    ny = pick_y.shape[1] // len(layers)
    first_y = (elem >> int(math.log2(nz // 4))) * 4
    y_at = lax.broadcasted_iota(jnp.int32, (ny, slots), 0)
    rows = []
    for b in range(5):
        row = first_y + b
        rows.append(jnp.where(row >= ny, row - ny, row))
    for i, a in enumerate(layers):
        for c in range(5):
            value = jnp.zeros((ny, slots), jnp.float32)
            for b in range(5):
                value = jnp.where(y_at == rows[b], weight(a, b, c), value)
            pick_y[c, i * ny : (i + 1) * ny] = value


def sample(values, pick_z, pick_y):
    rows = values.shape[0]
    slots = pick_y.shape[2]
    total = jnp.zeros((rows, slots), jnp.float32)
    for c in (0, 2, 4):
        some = min(2, 5 - c)
        picked = jnp.dot(
            values,
            pick_z[:, c * slots : (c + some) * slots],
            preferred_element_type=jnp.float32,
        )
        for k in range(some):
            total += picked[:, k * slots : (k + 1) * slots] * pick_y[c + k]
    return jnp.sum(jnp.sum(total.reshape(rows // 8, 8, slots), 0), 0, keepdims=True)


def split_three(v):
    high = v.astype(jnp.bfloat16).astype(jnp.float32)
    rest = v - high
    middle = rest.astype(jnp.bfloat16).astype(jnp.float32)
    return high, middle, rest - middle


def window_kernel(
    axes,
    sizes,
    now_hbm,
    vel_hbm,
    speed_hbm,
    src_hbm,
    elem_hbm,
    weight_hbm,
    left_hbm,
    right_hbm,
    station_hbm,
    wave_ref,
    blocks_ref,
    end_hbm,
    picked_ref,
    now_ref,
    vel_ref,
    speed_ref,
    src_ref,
    elem_ref,
    weight_ref,
    left_ref,
    right_ref,
    station_ref,
    field,
    acc,
    coef,
    x_own,
    x_left,
    pick_z,
    pick_y,
    pick_z_left,
    pick_y_left,
    hits,
    samp,
    setup_out,
    setup_in,
    send_v,
    send_p,
    recv_v,
    recv_p,
    recv_v2,
    recv_p2,
    send_a,
    send_b,
    recv_a,
    recv_b,
    send_x,
    x_right,
    x_left2,
    all_samp,
    load_sem,
    ssem,
    rsem,
    pair_ssem,
    pair_rsem,
    setup_sem,
    x_sem,
    all_sem,
    end_sem,
):
    planes, ny, nz = now_ref.shape
    slots = elem_ref.shape[1]
    n = sizes[0] * sizes[1]
    me = lax.axis_index(axes[0]) * sizes[1] + lax.axis_index(axes[1])

    loads = [
        pltpu.make_async_copy(src, dst, load_sem.at[i])
        for i, (src, dst) in enumerate(
            [
                (now_hbm, now_ref),
                (speed_hbm, speed_ref),
                (elem_hbm, elem_ref),
                (weight_hbm, weight_ref),
                (left_hbm, left_ref),
                (right_hbm, right_ref),
                (vel_hbm, vel_ref),
                (src_hbm, src_ref),
                (station_hbm, station_ref),
            ]
        )
    ]
    for load in loads:
        load.start()

    def device(j):
        return (j // sizes[1], j % sizes[1])

    right_dev = device((me + 1) % n)
    left_dev = device((me + n - 1) % n)
    right_dev2 = device((me + 2) % n)
    left_dev2 = device((me + n - 2) % n)

    barrier = pltpu.get_barrier_semaphore()

    @pl.loop(1, n)
    def _(off):
        pl.semaphore_signal(
            barrier, inc=1, device_id=device((me + off) % n), device_id_type=MESH
        )

    def to(src, dst, sems, at, target):
        return pltpu.make_async_remote_copy(
            src_ref=src,
            dst_ref=dst,
            send_sem=sems[0].at[at],
            recv_sem=sems[1].at[at],
            device_id=target,
            device_id_type=MESH,
        )

    def copies(t):
        sems = (ssem, rsem)
        return (
            to(send_v.at[t], recv_v.at[t], sems, (0, t), left_dev),
            to(send_p.at[t], recv_p.at[t], sems, (1, t), right_dev),
        )

    def far_copies(t, e):
        sems = (pair_ssem, pair_rsem)
        return (
            to(send_v.at[t], recv_v2.at[e], sems, (0, e), left_dev2),
            to(send_p.at[t], recv_p2.at[e], sems, (1, e), right_dev2),
        )

    def ahead_copies(e):
        sems = (pair_ssem, pair_rsem)
        return (
            to(send_a.at[e], recv_a.at[e], sems, (2, e), left_dev),
            to(send_b.at[e], recv_b.at[e], sems, (3, e), right_dev),
        )

    def x_copies():
        return (
            to(send_x, x_right, (x_sem.at[0], x_sem.at[1]), 0, left_dev),
            to(send_x, x_left2, (x_sem.at[0], x_sem.at[1]), 1, right_dev2),
        )

    def stage(t, u):
        send_v[t] = u[0].astype(jnp.bfloat16)
        total = u[0] * jnp.float32(K1[4, 0])
        for a in range(1, 4):
            total += u[a] * jnp.float32(K1[4, a])
        send_p[t] = total.astype(jnp.bfloat16)

    setup = pltpu.make_async_remote_copy(
        src_ref=setup_out,
        dst_ref=setup_in,
        send_sem=setup_sem.at[0],
        recv_sem=setup_sem.at[1],
        device_id=right_dev,
        device_id_type=MESH,
    )
    ey, ez = ny // 4, nz // 4
    setup_out[...] = jnp.zeros_like(setup_out)
    for load in loads[:4]:
        load.wait()
    elem = elem_ref[...]
    own_speed = speed_ref[0]
    setup_out[0:25] = weight_ref[100:125]
    setup_out[25:26] = elem.astype(jnp.float32)
    setup_out[32 : 32 + ey, 0:ez] = own_speed
    stage(0, [now_ref[p] for p in range(4)])

    pl.semaphore_wait(barrier, n - 1)
    setup.start()
    for copy in copies(0):
        copy.start()

    for load in loads[4:]:
        load.wait()
    for p in range(4):
        value = now_ref[p]
        field[0, p] = value
        field[1, p] = value - STEP_DT * vel_ref[p]
    left = left_ref[...]
    right = right_ref[...]
    own = speed_parts(own_speed, left, right)
    x_own[...] = own[0]
    send_x[...] = own[0].astype(jnp.bfloat16)
    for copy in x_copies():
        copy.start()
    write_coefficients(own[1:], coef, 1)
    write_pick_z(elem, pick_z)
    write_pick_y(
        elem,
        lambda a, b, c: weight_ref[25 * a + 5 * b + c : 25 * a + 5 * b + c + 1, :],
        range(4),
        pick_y,
        nz,
    )
    samp[...] = jnp.zeros_like(samp)

    setup.wait()
    before = speed_parts(setup_in[32 : 32 + ey, 0:ez], left, right)
    x_left[...] = before[0]
    write_coefficients([0.5 * (i + j) for i, j in zip(own[1:], before[1:])], coef, 0)

    def partial(t, slot):
        drive = wave_ref[t] * jnp.float32(STEP_DT * STEP_DT)
        for p in range(4):
            which = 0 if p == 0 else 1
            v = field[slot, p]
            total = 2.0 * v - field[1 - slot, p] + drive * src_ref[p] + coef[which, 16] * v
            along = field[slot, 0] * jnp.float32(K1[p, 0] / M1[p])
            for a in range(1, 4):
                along += field[slot, a] * jnp.float32(K1[p, a] / M1[p])
            total += x_own[...] * along
            if p == 0:
                total += x_left[...] * (v * jnp.float32(K1[4, 4] / M1[0]))
            for i, d in enumerate(OFFSETS[:8]):
                total += coef[which, i] * pltpu.roll(v, (-d) % ny, 0)
                total += coef[which, 8 + i] * pltpu.roll(v, (-d) % nz, 1)
            acc[p] = total

    def wait_halo(t):
        for copy in copies(t):
            copy.wait_recv()
        return recv_v[t].astype(jnp.float32), recv_p[t].astype(jnp.float32)

    def finish(halo, store):
        far, near = halo
        shared = x_own[...] * far
        out = []
        for p in range(4):
            total = acc[p] + shared * jnp.float32(K1[p, 4] / M1[p])
            if p == 0:
                total += x_left[...] * (near * jnp.float32(1.0 / M1[0]))
            store(p, total)
            out.append(total)
        return out

    def store_in(slot):
        def store(p, value):
            field[slot, p] = value

        return store

    def next_halo(t, e):
        for copy in (*far_copies(t, e), *ahead_copies(e)):
            copy.wait_recv()
        back = sum(K1[4, a] * K1[a, 4] / M1[a] for a in range(4))
        far = (
            recv_a[e].astype(jnp.float32)
            + x_right[...].astype(jnp.float32)
            * (recv_v2[e].astype(jnp.float32) * jnp.float32(K1[0, 4] / M1[0]))
            + x_own[...] * (send_p[t].astype(jnp.float32) * jnp.float32(1.0 / M1[0]))
        )
        near = (
            recv_b[e].astype(jnp.float32)
            + x_left[...] * (field[t % 2, 0] * jnp.float32(back))
            + x_left2[...].astype(jnp.float32)
            * (recv_p2[e].astype(jnp.float32) * jnp.float32(K1[4, 0] / M1[0]))
        )
        return far, near

    def take_samples(t, slot):
        values = jnp.concatenate([split_two(field[slot, p]) for p in range(4)], 0)
        samp[pl.ds(t, 1), :] = sample(values, pick_z, pick_y)
        samp[pl.ds(t + 8, 1), :] = sample(values[:ny], pick_z_left, pick_y_left)

    def two_steps(e, between):
        t = 1 + 2 * e
        for copy in (*copies(t), *far_copies(t, e)):
            copy.start()
        partial(t, 1)
        send_a[e] = acc[0].astype(jnp.bfloat16)
        total = acc[0] * jnp.float32(K1[4, 0])
        for a in range(1, 4):
            total += acc[a] * jnp.float32(K1[4, a])
        send_b[e] = total.astype(jnp.bfloat16)
        for copy in ahead_copies(e):
            copy.start()
        between()
        take_samples(t - 1, 0)
        take_samples(t, 1)
        finish(wait_halo(t), store_in(0))
        halo = next_halo(t, e)
        partial(t + 1, 0)
        stage(t + 2, finish(halo, store_in(1)))

    partial(0, 0)
    stage(1, finish(wait_halo(0), store_in(1)))

    def prepare():
        left_elem = setup_in[25:26].astype(jnp.int32)
        write_pick_z(left_elem, pick_z_left)
        write_pick_y(
            left_elem,
            lambda a, b, c: setup_in[5 * b + c : 5 * b + c + 1, :],
            range(4, 5),
            pick_y_left,
            nz,
        )
        for pair in range(hits.shape[0] // (2 * SB)):
            first = blocks_ref[pair, 0]
            second = blocks_ref[pair, 1]
            k = lax.broadcasted_iota(jnp.int32, (2 * SB, slots), 0)
            wanted = jnp.where(k < SB, first * SB + k, second * SB + k - SB)
            rows = slice(pair * 2 * SB, (pair + 1) * 2 * SB)
            for d in range(n):
                hit = jnp.where(wanted == station_ref[d : d + 1, :], 1.0, 0.0)
                hits[rows, d * slots : (d + 1) * slots] = hit.astype(jnp.bfloat16)
        for copy in x_copies():
            copy.wait_recv()

    two_steps(0, prepare)
    two_steps(1, lambda: None)

    last = NT - 1
    slot = last % 2
    for copy in copies(last):
        copy.start()
    take_samples(last - 1, 1 - slot)
    take_samples(last, slot)

    @pl.loop(1, n)
    def _(off):
        pltpu.make_async_remote_copy(
            src_ref=samp,
            dst_ref=all_samp.at[me],
            send_sem=all_sem.at[0],
            recv_sem=all_sem.at[1],
            device_id=device((me + off) % n),
            device_id_type=MESH,
        ).start()

    partial(last, slot)

    def store_end(p, value):
        acc[p] = value

    finish(wait_halo(last), store_end)
    put_end = pltpu.make_async_copy(acc, end_hbm, end_sem)
    put_end.start()
    whole = all_samp.at[pl.ds(0, n - 1)]
    everyone = pltpu.make_async_remote_copy(
        src_ref=whole,
        dst_ref=whole,
        send_sem=all_sem.at[0],
        recv_sem=all_sem.at[1],
        device_id=right_dev,
        device_id_type=MESH,
    )
    everyone.wait_recv()
    all_samp[me] = samp[...]
    parts = []
    for d in range(n):
        high, middle, low = split_three(all_samp[d, 0:8] + all_samp[(d + 1) % n, 8:16])
        parts.append(jnp.concatenate([high, middle, low, jnp.zeros_like(low)], 0))
    everything = jnp.concatenate(parts, 1).astype(jnp.bfloat16)
    for pair in range(hits.shape[0] // (2 * SB)):
        picked_ref[pair] = lax.dot_general(
            everything,
            hits[pair * 2 * SB : (pair + 1) * 2 * SB],
            (((1,), (1,)), ((), ())),
            preferred_element_type=jnp.float32,
        )
    everyone.wait_send()

    put_end.wait()
    for copy in x_copies():
        copy.wait_send()
    for t in (0, 1, 3, 5):
        for copy in copies(t):
            copy.wait_send()
    for e in range(2):
        for copy in (*far_copies(1 + 2 * e, e), *ahead_copies(e)):
            copy.wait_send()


def cross_kernel(picked_hbm, end_ref, table_ref, out_ref, final_ref, waves, picked_ref, sem):
    lanes = SB * SB
    pair = pl.program_id(0)
    chunk = pl.program_id(1)
    carry = pltpu.make_async_copy(end_ref, final_ref, sem.at[0])

    @pl.when((pair == 0) & (chunk == 0))
    def _():
        carry.start()

    @pl.when(chunk == 0)
    def _():
        fetch = pltpu.make_async_copy(picked_hbm.at[pair], picked_ref, sem.at[1])
        fetch.start()
        row = lax.broadcasted_iota(jnp.int32, (2 * SB, 2 * lanes), 0)
        lane = lax.broadcasted_iota(jnp.int32, (2 * SB, 2 * lanes), 1)
        source = jnp.where(lane < lanes, lane // SB, SB + lane % SB)
        spread = jnp.where(row == source, 1.0, 0.0).astype(jnp.bfloat16)
        fetch.wait()
        wide = jnp.dot(
            picked_ref[...].astype(jnp.bfloat16), spread, preferred_element_type=jnp.float32
        )
        high, middle, low = wide[0:8], wide[8:16], wide[16:24]
        waves[...] = jnp.concatenate([high, middle, high, low, high, middle], 0).astype(
            jnp.bfloat16
        )

    def spectrum(part):
        full = jnp.dot(table_ref[part], waves[...], preferred_element_type=jnp.float32)
        full = full.astype(jnp.bfloat16).astype(jnp.float32)
        return full[:, :lanes], full[:, lanes:]

    re_a, re_b = spectrum(0)
    im_a, im_b = spectrum(1)
    out_ref[0, 0] = ((re_a * re_b + im_a * im_b) * jnp.float32(1.0 / NT)).astype(jnp.bfloat16)
    out_ref[0, 1] = ((im_a * re_b - re_a * im_b) * jnp.float32(1.0 / NT)).astype(jnp.bfloat16)

    @pl.when((pair == pl.num_programs(0) - 1) & (chunk == pl.num_programs(1) - 1))
    def _():
        carry.wait()


def dft_table():
    angle = np.pi * (np.arange(F) + 0.5) / F
    phase = angle[:, None] * np.arange(8)[None, :]
    live = np.arange(8) < NT
    parts = []
    for table in (np.cos(phase) * live, -np.sin(phase) * live):
        table = table.astype(np.float32)
        high = table.astype(jnp.bfloat16).astype(np.float32)
        middle = (table - high).astype(jnp.bfloat16).astype(np.float32)
        low = table - high - middle
        parts.append(np.concatenate([high, high, middle, high, low, middle], 1))
    return jnp.asarray(np.stack(parts).astype(jnp.bfloat16))


def body(axes, sizes, *args):
    now, vel, speed, source, wavelet, elem, station, weight, blocks = args
    planes, ny, nz = now.shape
    slots = elem.shape[0]
    n = sizes[0] * sizes[1]
    pairs = blocks.shape[0]
    left, right = spread_matrices(ny, nz)
    f32, bf16 = jnp.float32, jnp.bfloat16
    anywhere = pl.BlockSpec(memory_space=pl.ANY)
    operands = (
        now,
        vel,
        speed,
        source,
        elem.reshape(1, slots),
        weight,
        jnp.asarray(left),
        jnp.asarray(right),
        station.reshape(n, slots),
    )
    end, picked = pl.pallas_call(
        functools.partial(window_kernel, axes, sizes),
        out_shape=(
            jax.ShapeDtypeStruct(now.shape, f32),
            jax.ShapeDtypeStruct((pairs, 32, 2 * SB), f32),
        ),
        in_specs=[anywhere] * len(operands) + [pl.BlockSpec(memory_space=pltpu.SMEM)] * 2,
        out_specs=(anywhere, pl.BlockSpec(memory_space=pltpu.VMEM)),
        scratch_shapes=[pltpu.VMEM(x.shape, x.dtype) for x in operands]
        + [
            pltpu.VMEM((2, planes, ny, nz), f32),
            pltpu.VMEM((planes, ny, nz), f32),
            pltpu.VMEM((2, 17, ny, nz), f32),
            pltpu.VMEM((ny, nz), f32),
            pltpu.VMEM((ny, nz), f32),
            pltpu.VMEM((2 * nz, 5 * slots), bf16),
            pltpu.VMEM((5, planes * ny, slots), f32),
            pltpu.VMEM((2 * nz, 5 * slots), bf16),
            pltpu.VMEM((5, ny, slots), f32),
            pltpu.VMEM((pairs * 2 * SB, n * slots), bf16),
            pltpu.VMEM((16, slots), f32),
            pltpu.VMEM((32 + ny // 4, slots), f32),
            pltpu.VMEM((32 + ny // 4, slots), f32),
            pltpu.VMEM((NT, ny, nz), bf16),
            pltpu.VMEM((NT, ny, nz), bf16),
            pltpu.VMEM((NT, ny, nz), bf16),
            pltpu.VMEM((NT, ny, nz), bf16),
        ]
        + [pltpu.VMEM((2, ny, nz), bf16)] * 6
        + [pltpu.VMEM((ny, nz), bf16)] * 3
        + [
            pltpu.VMEM((n, 16, slots), f32),
            pltpu.SemaphoreType.DMA((len(operands),)),
            pltpu.SemaphoreType.DMA((2, NT)),
            pltpu.SemaphoreType.DMA((2, NT)),
            pltpu.SemaphoreType.DMA((4, 2)),
            pltpu.SemaphoreType.DMA((4, 2)),
            pltpu.SemaphoreType.DMA((2,)),
            pltpu.SemaphoreType.DMA((2, 2)),
            pltpu.SemaphoreType.DMA((2,)),
            pltpu.SemaphoreType.DMA(()),
        ],
        compiler_params=pltpu.CompilerParams(
            collective_id=0, has_side_effects=True, vmem_limit_bytes=56 * 2**20
        ),
        name="window",
    )(*operands, wavelet, blocks)
    chunk = F // 2
    cross, final = pl.pallas_call(
        cross_kernel,
        out_shape=(
            jax.ShapeDtypeStruct((pairs, 2, F, SB * SB), bf16),
            jax.ShapeDtypeStruct(now.shape, f32),
        ),
        grid=(pairs, F // chunk),
        in_specs=[
            anywhere,
            anywhere,
            pl.BlockSpec((2, chunk, 48), lambda p, f: (0, f, 0)),
        ],
        out_specs=(
            pl.BlockSpec((1, 2, chunk, SB * SB), lambda p, f: (p, 0, f, 0)),
            anywhere,
        ),
        scratch_shapes=[
            pltpu.VMEM((48, 2 * SB * SB), bf16),
            pltpu.VMEM((32, 2 * SB), f32),
            pltpu.SemaphoreType.DMA((2,)),
        ],
        compiler_params=pltpu.CompilerParams(vmem_limit_bytes=56 * 2**20),
        name="cross",
    )(picked, end, dft_table())
    return final, cross


def solution(mesh):
    axes = ("pair", "bulk")
    sizes = tuple(mesh.shape[a] for a in axes)
    split = P(axes, None, None)
    in_specs = (
        split,
        split,
        split,
        split,
        P(),
        P(axes),
        P(),
        P(None, axes),
        P(axes, None),
    )
    return jax.shard_map(
        functools.partial(body, axes, sizes),
        mesh=mesh,
        in_specs=in_specs,
        out_specs=(split, P(axes, None, None, None)),
        check_vma=False,
    )
```

```python
import functools
import math

import jax
import jax.numpy as jnp
import numpy as np
from jax import lax
from jax.experimental import pallas as pl
from jax.experimental.pallas import tpu as pltpu
from jax.sharding import PartitionSpec as P

NT = 6
F = 256
SB = 32
STEP_DT = 0.04
MESH = pl.DeviceIdType.MESH


def gll_tables():
    points = np.array([-1.0, -math.sqrt(3.0 / 7.0), 0.0, math.sqrt(3.0 / 7.0), 1.0])
    quadrature = np.array([0.1, 49.0 / 90.0, 32.0 / 45.0, 49.0 / 90.0, 0.1])
    factor = np.array(
        [np.prod([points[i] - points[j] for j in range(5) if j != i]) for i in range(5)]
    )
    derivative = np.zeros((5, 5))
    for i in range(5):
        for j in range(5):
            if i != j:
                derivative[i, j] = factor[i] / (factor[j] * (points[i] - points[j]))
        derivative[i, i] = -np.sum(derivative[i])
    return derivative, quadrature


DERIV, QUAD = gll_tables()
K1 = DERIV.T @ np.diag(QUAD) @ DERIV
M1 = np.array([0.2, QUAD[1], QUAD[2], QUAD[3]])
OFFSETS = (-4, -3, -2, -1, 1, 2, 3, 4, 0)


def spread_matrices(ny, nz):
    ey, ez = ny // 4, nz // 4
    wy = np.zeros((ny, ey))
    wz = np.zeros((ez, nz))
    for e in range(ey):
        for b in range(5):
            r = (4 * e + b) % ny
            wy[r, e] += QUAD[b] / M1[r % 4]
    for e in range(ez):
        for c in range(5):
            r = 4 * e + c
            if r < nz:
                wz[e, r] += QUAD[c] / (0.1 if r == 0 else M1[r % 4])
    own_y = np.zeros((ny, ey))
    prev_y = np.zeros((ny, ey))
    own_z = np.zeros((ez, nz))
    prev_z = np.zeros((ez, nz))
    for r in range(ny):
        own_y[r, r // 4] = 1
        prev_y[r, (r // 4 - 1) % ey] = 1
    for c in range(nz):
        own_z[c // 4, c] = 1
        if c >= 4:
            prev_z[c // 4 - 1, c] = 1
    left = np.concatenate([wy, own_y, prev_y], 0).astype(np.float32)
    right = np.concatenate([wz, own_z, prev_z], 1).astype(np.float32)
    return left, right


def own_factor(b, d):
    return K1[b, b + d] / M1[b] if 0 <= b + d <= 4 else 0.0


def prev_factor(b, d):
    return K1[4, 4 + d] / M1[0] if b == 0 and -4 <= d <= 0 else 0.0


def by_position(position, values):
    out = jnp.full(position.shape, values[0], jnp.float32)
    for b in range(1, 4):
        out = jnp.where(position == b, jnp.float32(values[b]), out)
    return out


def high_low(v):
    high = v.astype(jnp.bfloat16).astype(jnp.float32)
    return high, v - high


def spread_right(v, constant):
    both = jnp.concatenate(high_low(v), 1).astype(jnp.bfloat16)
    twice = jnp.concatenate([constant, constant], 0).astype(jnp.bfloat16)
    return jnp.dot(both, twice, preferred_element_type=jnp.float32)


def spread_left(constant, v):
    both = jnp.concatenate(high_low(v), 0).astype(jnp.bfloat16)
    twice = jnp.concatenate([constant, constant], 1).astype(jnp.bfloat16)
    return jnp.dot(twice, both, preferred_element_type=jnp.float32)


def speed_parts(speed, left, right):
    ny, nz = left.shape[0] // 3, right.shape[1] // 3
    scale = -STEP_DT * STEP_DT
    rows = spread_left(left, spread_right(speed, right[:, :nz]) * scale)
    cols = spread_right(spread_left(left[:ny], speed) * scale, right[:, nz:])
    return rows[:ny], rows[ny : 2 * ny], rows[2 * ny :], cols[:, :nz], cols[:, nz:]


def write_coefficients(parts, coef, which):
    row_own, row_prev, col_own, col_prev = parts
    ny, nz = row_own.shape
    row = lax.broadcasted_iota(jnp.int32, (8, nz), 0) & 3
    lane = lax.broadcasted_iota(jnp.int32, (8, nz), 1)
    col = lane & 3

    def times(values, tile):
        return (values.reshape(ny // 8, 8, nz) * tile[None]).reshape(ny, nz)

    for i, d in enumerate(OFFSETS):
        y_part = times(row_own, by_position(row, [own_factor(b, d) for b in range(4)]))
        if d <= 0:
            y_part += times(row_prev, by_position(row, [prev_factor(b, d) for b in range(4)]))
        z_own = by_position(col, [own_factor(b, d) for b in range(4)])
        z_own = jnp.where(lane == 0, jnp.float32(own_factor(0, d) * M1[0] / 0.1), z_own)
        z_own = jnp.where(lane + d >= nz, 0.0, z_own)
        z_part = times(col_own, z_own)
        if d <= 0:
            z_part += times(col_prev, by_position(col, [prev_factor(b, d) for b in range(4)]))
        if d == 0:
            coef[which, 16] = y_part + z_part
        else:
            coef[which, i] = y_part
            coef[which, 8 + i] = z_part


def split_two(v):
    high = v.astype(jnp.bfloat16)
    low = (v - high.astype(jnp.float32)).astype(jnp.bfloat16)
    return jnp.concatenate([high, low], 1)


def write_pick_z(elem, pick_z):
    slots = elem.shape[1]
    nz = pick_z.shape[0] // 2
    first_z = (elem & (nz // 4 - 1)) * 4
    z_at = lax.broadcasted_iota(jnp.int32, (nz, slots), 0)
    for c in range(5):
        hit = jnp.where(z_at == first_z + c, 1.0, 0.0).astype(jnp.bfloat16)
        pick_z[0:nz, c * slots : (c + 1) * slots] = hit
        pick_z[nz : 2 * nz, c * slots : (c + 1) * slots] = hit


def write_pick_y(elem, weight, layers, pick_y, nz):
    slots = elem.shape[1]
    ny = pick_y.shape[1] // len(layers)
    first_y = (elem >> int(math.log2(nz // 4))) * 4
    y_at = lax.broadcasted_iota(jnp.int32, (ny, slots), 0)
    rows = []
    for b in range(5):
        row = first_y + b
        rows.append(jnp.where(row >= ny, row - ny, row))
    for i, a in enumerate(layers):
        for c in range(5):
            value = jnp.zeros((ny, slots), jnp.float32)
            for b in range(5):
                value = jnp.where(y_at == rows[b], weight(a, b, c), value)
            pick_y[c, i * ny : (i + 1) * ny] = value


def sample(values, pick_z, pick_y):
    rows = values.shape[0]
    slots = pick_y.shape[2]
    total = jnp.zeros((rows, slots), jnp.float32)
    for c in (0, 2, 4):
        some = min(2, 5 - c)
        picked = jnp.dot(
            values,
            pick_z[:, c * slots : (c + some) * slots],
            preferred_element_type=jnp.float32,
        )
        for k in range(some):
            total += picked[:, k * slots : (k + 1) * slots] * pick_y[c + k]
    return jnp.sum(jnp.sum(total.reshape(rows // 8, 8, slots), 0), 0, keepdims=True)


def split_three(v):
    high = v.astype(jnp.bfloat16).astype(jnp.float32)
    rest = v - high
    middle = rest.astype(jnp.bfloat16).astype(jnp.float32)
    return high, middle, rest - middle


def window_kernel(
    axes,
    sizes,
    now_hbm,
    vel_hbm,
    speed_hbm,
    src_hbm,
    elem_hbm,
    weight_hbm,
    left_hbm,
    right_hbm,
    station_hbm,
    wave_ref,
    blocks_ref,
    end_hbm,
    picked_ref,
    now_ref,
    vel_ref,
    speed_ref,
    src_ref,
    elem_ref,
    weight_ref,
    left_ref,
    right_ref,
    station_ref,
    field,
    acc,
    coef,
    x_own,
    x_left,
    pick_z,
    pick_y,
    pick_z_left,
    pick_y_left,
    hits,
    samp,
    setup_out,
    setup_in,
    send_v,
    send_p,
    recv_v,
    recv_p,
    recv_v2,
    recv_p2,
    send_a,
    send_b,
    recv_a,
    recv_b,
    send_x,
    x_right,
    x_left2,
    all_samp,
    load_sem,
    ssem,
    rsem,
    pair_ssem,
    pair_rsem,
    setup_sem,
    x_sem,
    all_sem,
    end_sem,
):
    planes, ny, nz = now_ref.shape
    slots = elem_ref.shape[1]
    n = sizes[0] * sizes[1]
    me = lax.axis_index(axes[0]) * sizes[1] + lax.axis_index(axes[1])

    loads = [
        pltpu.make_async_copy(src, dst, load_sem.at[i])
        for i, (src, dst) in enumerate(
            [
                (now_hbm, now_ref),
                (speed_hbm, speed_ref),
                (elem_hbm, elem_ref),
                (weight_hbm, weight_ref),
                (left_hbm, left_ref),
                (right_hbm, right_ref),
                (vel_hbm, vel_ref),
                (src_hbm, src_ref),
                (station_hbm, station_ref),
            ]
        )
    ]
    for load in loads[:4]:
        load.start()

    def device(off):
        j = me + off
        j = jnp.where(j >= n, j - n, j)
        return (lax.div(j, sizes[1]), lax.rem(j, sizes[1]))

    right_dev = device(1)
    left_dev = device(n - 1)
    right_dev2 = device(2)
    left_dev2 = device(n - 2)

    barrier = pltpu.get_barrier_semaphore()

    for off in range(1, n):
        pl.semaphore_signal(barrier, inc=1, device_id=device(off), device_id_type=MESH)
    for load in loads[4:]:
        load.start()

    def to(src, dst, sems, at, target):
        return pltpu.make_async_remote_copy(
            src_ref=src,
            dst_ref=dst,
            send_sem=sems[0].at[at],
            recv_sem=sems[1].at[at],
            device_id=target,
            device_id_type=MESH,
        )

    def copies(t):
        sems = (ssem, rsem)
        return (
            to(send_v.at[t], recv_v.at[t], sems, (0, t), left_dev),
            to(send_p.at[t], recv_p.at[t], sems, (1, t), right_dev),
        )

    def far_copies(t, e):
        sems = (pair_ssem, pair_rsem)
        return (
            to(send_v.at[t], recv_v2.at[e], sems, (0, e), left_dev2),
            to(send_p.at[t], recv_p2.at[e], sems, (1, e), right_dev2),
        )

    def ahead_copies(e):
        sems = (pair_ssem, pair_rsem)
        return (
            to(send_a.at[e], recv_a.at[e], sems, (2, e), left_dev),
            to(send_b.at[e], recv_b.at[e], sems, (3, e), right_dev),
        )

    def x_copies():
        return (
            to(send_x, x_right, (x_sem.at[0], x_sem.at[1]), 0, left_dev),
            to(send_x, x_left2, (x_sem.at[0], x_sem.at[1]), 1, right_dev2),
        )

    def stage(t, u):
        send_v[t] = u[0].astype(jnp.bfloat16)
        total = u[0] * jnp.float32(K1[4, 0])
        for a in range(1, 4):
            total += u[a] * jnp.float32(K1[4, a])
        send_p[t] = total.astype(jnp.bfloat16)

    setup = pltpu.make_async_remote_copy(
        src_ref=setup_out,
        dst_ref=setup_in,
        send_sem=setup_sem.at[0],
        recv_sem=setup_sem.at[1],
        device_id=right_dev,
        device_id_type=MESH,
    )
    ey, ez = ny // 4, nz // 4
    setup_out[...] = jnp.zeros_like(setup_out)
    for load in loads[:4]:
        load.wait()
    elem = elem_ref[...]
    own_speed = speed_ref[0]
    setup_out[0:25] = weight_ref[100:125]
    setup_out[25:26] = elem.astype(jnp.float32)
    setup_out[32 : 32 + ey, 0:ez] = own_speed
    stage(0, [now_ref[p] for p in range(4)])

    pl.semaphore_wait(barrier, n - 1)
    setup.start()
    for copy in copies(0):
        copy.start()

    for load in loads[4:]:
        load.wait()
    for p in range(4):
        value = now_ref[p]
        field[0, p] = value
        field[1, p] = value - STEP_DT * vel_ref[p]
    left = left_ref[...]
    right = right_ref[...]
    own = speed_parts(own_speed, left, right)
    x_own[...] = own[0]
    send_x[...] = own[0].astype(jnp.bfloat16)
    for copy in x_copies():
        copy.start()
    write_coefficients(own[1:], coef, 1)
    write_pick_z(elem, pick_z)
    write_pick_y(
        elem,
        lambda a, b, c: weight_ref[25 * a + 5 * b + c : 25 * a + 5 * b + c + 1, :],
        range(4),
        pick_y,
        nz,
    )
    samp[...] = jnp.zeros_like(samp)

    def partial(t, slot, planes=range(4)):
        drive = wave_ref[t] * jnp.float32(STEP_DT * STEP_DT)
        for p in planes:
            which = 0 if p == 0 else 1
            v = field[slot, p]
            total = 2.0 * v - field[1 - slot, p] + drive * src_ref[p] + coef[which, 16] * v
            along = field[slot, 0] * jnp.float32(K1[p, 0] / M1[p])
            for a in range(1, 4):
                along += field[slot, a] * jnp.float32(K1[p, a] / M1[p])
            total += x_own[...] * along
            if p == 0:
                total += x_left[...] * (v * jnp.float32(K1[4, 4] / M1[0]))
            for i, d in enumerate(OFFSETS[:8]):
                total += coef[which, i] * pltpu.roll(v, (-d) % ny, 0)
                total += coef[which, 8 + i] * pltpu.roll(v, (-d) % nz, 1)
            acc[p] = total

    partial(0, 0, range(1, 4))
    setup.wait()
    before = speed_parts(setup_in[32 : 32 + ey, 0:ez], left, right)
    x_left[...] = before[0]
    write_coefficients([0.5 * (i + j) for i, j in zip(own[1:], before[1:])], coef, 0)
    partial(0, 0, range(1))

    def wait_halo(t):
        for copy in copies(t):
            copy.wait_recv()
        return recv_v[t].astype(jnp.float32), recv_p[t].astype(jnp.float32)

    def finish(halo, store):
        far, near = halo
        shared = x_own[...] * far
        out = []
        for p in range(4):
            total = acc[p] + shared * jnp.float32(K1[p, 4] / M1[p])
            if p == 0:
                total += x_left[...] * (near * jnp.float32(1.0 / M1[0]))
            store(p, total)
            out.append(total)
        return out

    def store_in(slot):
        def store(p, value):
            field[slot, p] = value

        return store

    def next_halo(t, e):
        for copy in (*far_copies(t, e), *ahead_copies(e)):
            copy.wait_recv()
        back = sum(K1[4, a] * K1[a, 4] / M1[a] for a in range(4))
        far = (
            recv_a[e].astype(jnp.float32)
            + x_right[...].astype(jnp.float32)
            * (recv_v2[e].astype(jnp.float32) * jnp.float32(K1[0, 4] / M1[0]))
            + x_own[...] * (send_p[t].astype(jnp.float32) * jnp.float32(1.0 / M1[0]))
        )
        near = (
            recv_b[e].astype(jnp.float32)
            + x_left[...] * (field[t % 2, 0] * jnp.float32(back))
            + x_left2[...].astype(jnp.float32)
            * (recv_p2[e].astype(jnp.float32) * jnp.float32(K1[4, 0] / M1[0]))
        )
        return far, near

    def take_samples(t, slot):
        values = jnp.concatenate([split_two(field[slot, p]) for p in range(4)], 0)
        samp[pl.ds(t, 1), :] = sample(values, pick_z, pick_y)
        samp[pl.ds(t + 8, 1), :] = sample(values[:ny], pick_z_left, pick_y_left)

    def two_steps(e, between):
        t = 1 + 2 * e
        for copy in (*copies(t), *far_copies(t, e)):
            copy.start()
        partial(t, 1)
        send_a[e] = acc[0].astype(jnp.bfloat16)
        total = acc[0] * jnp.float32(K1[4, 0])
        for a in range(1, 4):
            total += acc[a] * jnp.float32(K1[4, a])
        send_b[e] = total.astype(jnp.bfloat16)
        for copy in ahead_copies(e):
            copy.start()
        between()
        take_samples(t - 1, 0)
        take_samples(t, 1)
        finish(wait_halo(t), store_in(0))
        halo = next_halo(t, e)
        partial(t + 1, 0)
        stage(t + 2, finish(halo, store_in(1)))

    stage(1, finish(wait_halo(0), store_in(1)))

    def prepare():
        left_elem = setup_in[25:26].astype(jnp.int32)
        write_pick_z(left_elem, pick_z_left)
        write_pick_y(
            left_elem,
            lambda a, b, c: setup_in[5 * b + c : 5 * b + c + 1, :],
            range(4, 5),
            pick_y_left,
            nz,
        )
        for pair in range(hits.shape[0] // (2 * SB)):
            first = blocks_ref[pair, 0]
            second = blocks_ref[pair, 1]
            k = lax.broadcasted_iota(jnp.int32, (2 * SB, slots), 0)
            wanted = jnp.where(k < SB, first * SB + k, second * SB + k - SB)
            rows = slice(pair * 2 * SB, (pair + 1) * 2 * SB)
            for d in range(n):
                hit = jnp.where(wanted == station_ref[d : d + 1, :], 1.0, 0.0)
                hits[rows, d * slots : (d + 1) * slots] = hit.astype(jnp.bfloat16)
        for copy in x_copies():
            copy.wait_recv()

    two_steps(0, prepare)
    two_steps(1, lambda: None)

    last = NT - 1
    slot = last % 2
    for copy in copies(last):
        copy.start()
    take_samples(last - 1, 1 - slot)
    take_samples(last, slot)

    for off in range(1, n):
        pltpu.make_async_remote_copy(
            src_ref=samp,
            dst_ref=all_samp.at[me],
            send_sem=all_sem.at[0],
            recv_sem=all_sem.at[1],
            device_id=device(off),
            device_id_type=MESH,
        ).start()

    partial(last, slot)

    def store_end(p, value):
        acc[p] = value

    finish(wait_halo(last), store_end)
    put_end = pltpu.make_async_copy(acc, end_hbm, end_sem)
    put_end.start()
    whole = all_samp.at[pl.ds(0, n - 1)]
    everyone = pltpu.make_async_remote_copy(
        src_ref=whole,
        dst_ref=whole,
        send_sem=all_sem.at[0],
        recv_sem=all_sem.at[1],
        device_id=right_dev,
        device_id_type=MESH,
    )
    everyone.wait_recv()
    all_samp[me] = samp[...]
    parts = []
    for d in range(n):
        high, middle, low = split_three(all_samp[d, 0:8] + all_samp[(d + 1) % n, 8:16])
        parts.append(jnp.concatenate([high, middle, low, jnp.zeros_like(low)], 0))
    everything = jnp.concatenate(parts, 1).astype(jnp.bfloat16)
    for pair in range(hits.shape[0] // (2 * SB)):
        picked_ref[pair] = lax.dot_general(
            everything,
            hits[pair * 2 * SB : (pair + 1) * 2 * SB],
            (((1,), (1,)), ((), ())),
            preferred_element_type=jnp.float32,
        )
    everyone.wait_send()

    put_end.wait()
    for copy in x_copies():
        copy.wait_send()
    for t in (0, 1, 3, 5):
        for copy in copies(t):
            copy.wait_send()
    for e in range(2):
        for copy in (*far_copies(1 + 2 * e, e), *ahead_copies(e)):
            copy.wait_send()


def cross_kernel(picked_hbm, end_ref, table_ref, out_ref, final_ref, waves, picked_ref, held, sem):
    lanes = SB * SB
    pair = pl.program_id(0)
    chunk = pl.program_id(1)
    take = pltpu.make_async_copy(end_ref, held, sem.at[0])
    give = pltpu.make_async_copy(held, final_ref, sem.at[2])

    @pl.when(chunk == 0)
    def _():
        fetch = pltpu.make_async_copy(picked_hbm.at[pair], picked_ref, sem.at[1])
        fetch.start()

        @pl.when(pair == 0)
        def _():
            take.start()

        row = lax.broadcasted_iota(jnp.int32, (2 * SB, 2 * lanes), 0)
        lane = lax.broadcasted_iota(jnp.int32, (2 * SB, 2 * lanes), 1)
        source = jnp.where(lane < lanes, lane // SB, SB + lane % SB)
        spread = jnp.where(row == source, 1.0, 0.0).astype(jnp.bfloat16)
        fetch.wait()
        wide = jnp.dot(
            picked_ref[...].astype(jnp.bfloat16), spread, preferred_element_type=jnp.float32
        )
        high, middle, low = wide[0:8], wide[8:16], wide[16:24]
        waves[...] = jnp.concatenate([high, middle, high, low, high, middle], 0).astype(
            jnp.bfloat16
        )

    def spectrum(part):
        full = jnp.dot(table_ref[part], waves[...], preferred_element_type=jnp.float32)
        full = full.astype(jnp.bfloat16).astype(jnp.float32)
        return full[:, :lanes], full[:, lanes:]

    @pl.when((pair == 0) & (chunk == 0))
    def _():
        take.wait()
        give.start()

    re_a, re_b = spectrum(0)
    im_a, im_b = spectrum(1)
    out_ref[0, 0] = ((re_a * re_b + im_a * im_b) * jnp.float32(1.0 / NT)).astype(jnp.bfloat16)
    out_ref[0, 1] = ((im_a * re_b - re_a * im_b) * jnp.float32(1.0 / NT)).astype(jnp.bfloat16)

    @pl.when((pair == pl.num_programs(0) - 1) & (chunk == pl.num_programs(1) - 1))
    def _():
        give.wait()


def dft_table():
    angle = np.pi * (np.arange(F) + 0.5) / F
    phase = angle[:, None] * np.arange(8)[None, :]
    live = np.arange(8) < NT
    parts = []
    for table in (np.cos(phase) * live, -np.sin(phase) * live):
        table = table.astype(np.float32)
        high = table.astype(jnp.bfloat16).astype(np.float32)
        middle = (table - high).astype(jnp.bfloat16).astype(np.float32)
        low = table - high - middle
        parts.append(np.concatenate([high, high, middle, high, low, middle], 1))
    return jnp.asarray(np.stack(parts).astype(jnp.bfloat16))


def body(axes, sizes, *args):
    now, vel, speed, source, wavelet, elem, station, weight, blocks = args
    planes, ny, nz = now.shape
    slots = elem.shape[0]
    n = sizes[0] * sizes[1]
    pairs = blocks.shape[0]
    left, right = spread_matrices(ny, nz)
    f32, bf16 = jnp.float32, jnp.bfloat16
    anywhere = pl.BlockSpec(memory_space=pl.ANY)
    operands = (
        now,
        vel,
        speed,
        source,
        elem.reshape(1, slots),
        weight,
        jnp.asarray(left),
        jnp.asarray(right),
        station.reshape(n, slots),
    )
    end, picked = pl.pallas_call(
        functools.partial(window_kernel, axes, sizes),
        out_shape=(
            jax.ShapeDtypeStruct(now.shape, f32),
            jax.ShapeDtypeStruct((pairs, 32, 2 * SB), f32),
        ),
        in_specs=[anywhere] * len(operands) + [pl.BlockSpec(memory_space=pltpu.SMEM)] * 2,
        out_specs=(anywhere, pl.BlockSpec(memory_space=pltpu.VMEM)),
        scratch_shapes=[pltpu.VMEM(x.shape, x.dtype) for x in operands]
        + [
            pltpu.VMEM((2, planes, ny, nz), f32),
            pltpu.VMEM((planes, ny, nz), f32),
            pltpu.VMEM((2, 17, ny, nz), f32),
            pltpu.VMEM((ny, nz), f32),
            pltpu.VMEM((ny, nz), f32),
            pltpu.VMEM((2 * nz, 5 * slots), bf16),
            pltpu.VMEM((5, planes * ny, slots), f32),
            pltpu.VMEM((2 * nz, 5 * slots), bf16),
            pltpu.VMEM((5, ny, slots), f32),
            pltpu.VMEM((pairs * 2 * SB, n * slots), bf16),
            pltpu.VMEM((16, slots), f32),
            pltpu.VMEM((32 + ny // 4, slots), f32),
            pltpu.VMEM((32 + ny // 4, slots), f32),
            pltpu.VMEM((NT, ny, nz), bf16),
            pltpu.VMEM((NT, ny, nz), bf16),
            pltpu.VMEM((NT, ny, nz), bf16),
            pltpu.VMEM((NT, ny, nz), bf16),
        ]
        + [pltpu.VMEM((2, ny, nz), bf16)] * 6
        + [pltpu.VMEM((ny, nz), bf16)] * 3
        + [
            pltpu.VMEM((n, 16, slots), f32),
            pltpu.SemaphoreType.DMA((len(operands),)),
            pltpu.SemaphoreType.DMA((2, NT)),
            pltpu.SemaphoreType.DMA((2, NT)),
            pltpu.SemaphoreType.DMA((4, 2)),
            pltpu.SemaphoreType.DMA((4, 2)),
            pltpu.SemaphoreType.DMA((2,)),
            pltpu.SemaphoreType.DMA((2, 2)),
            pltpu.SemaphoreType.DMA((2,)),
            pltpu.SemaphoreType.DMA(()),
        ],
        compiler_params=pltpu.CompilerParams(
            collective_id=0, has_side_effects=True, vmem_limit_bytes=56 * 2**20
        ),
        name="window",
    )(*operands, wavelet, blocks)
    chunk = F // 2
    cross, final = pl.pallas_call(
        cross_kernel,
        out_shape=(
            jax.ShapeDtypeStruct((pairs, 2, F, SB * SB), bf16),
            jax.ShapeDtypeStruct(now.shape, f32),
        ),
        grid=(pairs, F // chunk),
        in_specs=[
            anywhere,
            anywhere,
            pl.BlockSpec((2, chunk, 48), lambda p, f: (0, f, 0)),
        ],
        out_specs=(
            pl.BlockSpec((1, 2, chunk, SB * SB), lambda p, f: (p, 0, f, 0)),
            anywhere,
        ),
        scratch_shapes=[
            pltpu.VMEM((48, 2 * SB * SB), bf16),
            pltpu.VMEM((32, 2 * SB), f32),
            pltpu.VMEM(now.shape, f32),
            pltpu.SemaphoreType.DMA((3,)),
        ],
        compiler_params=pltpu.CompilerParams(vmem_limit_bytes=56 * 2**20),
        name="cross",
    )(picked, end, dft_table())
    return final, cross


def solution(mesh):
    axes = ("pair", "bulk")
    sizes = tuple(mesh.shape[a] for a in axes)
    split = P(axes, None, None)
    in_specs = (
        split,
        split,
        split,
        split,
        P(),
        P(axes),
        P(),
        P(None, axes),
        P(axes, None),
    )
    return jax.shard_map(
        functools.partial(body, axes, sizes),
        mesh=mesh,
        in_specs=in_specs,
        out_specs=(split, P(axes, None, None, None)),
        check_vma=False,
    )
```

```python
import functools
import math

import jax
import jax.numpy as jnp
import numpy as np
from jax import lax
from jax.experimental import pallas as pl
from jax.experimental.pallas import tpu as pltpu
from jax.sharding import PartitionSpec as P

NT = 6
F = 256
SB = 32
STEP_DT = 0.04
MESH = pl.DeviceIdType.MESH


def gll_tables():
    points = np.array([-1.0, -math.sqrt(3.0 / 7.0), 0.0, math.sqrt(3.0 / 7.0), 1.0])
    quadrature = np.array([0.1, 49.0 / 90.0, 32.0 / 45.0, 49.0 / 90.0, 0.1])
    factor = np.array(
        [np.prod([points[i] - points[j] for j in range(5) if j != i]) for i in range(5)]
    )
    derivative = np.zeros((5, 5))
    for i in range(5):
        for j in range(5):
            if i != j:
                derivative[i, j] = factor[i] / (factor[j] * (points[i] - points[j]))
        derivative[i, i] = -np.sum(derivative[i])
    return derivative, quadrature


DERIV, QUAD = gll_tables()
K1 = DERIV.T @ np.diag(QUAD) @ DERIV
M1 = np.array([0.2, QUAD[1], QUAD[2], QUAD[3]])


def spread_matrices(ny, nz):
    ey, ez = ny // 4, nz // 4
    wy = np.zeros((ny, ey))
    wz = np.zeros((ez, nz))
    for e in range(ey):
        for b in range(5):
            r = (4 * e + b) % ny
            wy[r, e] += QUAD[b] / M1[r % 4]
    for e in range(ez):
        for c in range(5):
            r = 4 * e + c
            if r < nz:
                wz[e, r] += QUAD[c] / (0.1 if r == 0 else M1[r % 4])
    own_y = np.zeros((ny, ey))
    prev_y = np.zeros((ny, ey))
    own_z = np.zeros((ez, nz))
    prev_z = np.zeros((ez, nz))
    for r in range(ny):
        own_y[r, r // 4] = 1
        prev_y[r, (r // 4 - 1) % ey] = 1
    for c in range(nz):
        own_z[c // 4, c] = 1
        if c >= 4:
            prev_z[c // 4 - 1, c] = 1
    left = np.concatenate([wy, own_y, prev_y], 0).astype(np.float32)
    right = np.concatenate([wz, own_z, prev_z], 1).astype(np.float32)
    return left, right


def own_factor(b, d):
    return K1[b, b + d] / M1[b] if 0 <= b + d <= 4 else 0.0


def prev_factor(b, d):
    return K1[4, 4 + d] / M1[0] if b == 0 and -4 <= d <= 0 else 0.0


def stencil_matrices(ny, nz):
    along_y = np.zeros((2 * ny, ny))
    along_z = np.zeros((nz, 2 * nz))
    for r in range(ny):
        for d in range(-4, 5):
            along_y[r, (r + d) % ny] += own_factor(r % 4, d)
            along_y[ny + r, (r + d) % ny] += prev_factor(r % 4, d)
    for c in range(nz):
        for d in range(-4, 5):
            if 0 <= c + d < nz:
                along_z[c + d, c] += own_factor(c % 4, d) * (M1[0] / 0.1 if c == 0 else 1.0)
                along_z[c + d, nz + c] += prev_factor(c % 4, d) if c >= 4 else 0.0
    out = []
    for matrix, axis in ((along_y, 1), (along_z, 0)):
        matrix = matrix.astype(np.float32)
        high = matrix.astype(jnp.bfloat16)
        low = (matrix - high.astype(np.float32)).astype(jnp.bfloat16)
        out.append(jnp.asarray(np.concatenate([high, high, low], axis)))
    return out


def high_low(v):
    high = v.astype(jnp.bfloat16).astype(jnp.float32)
    return high, v - high


def spread_right(v, constant):
    both = jnp.concatenate(high_low(v), 1).astype(jnp.bfloat16)
    twice = jnp.concatenate([constant, constant], 0).astype(jnp.bfloat16)
    return jnp.dot(both, twice, preferred_element_type=jnp.float32)


def spread_left(constant, v):
    both = jnp.concatenate(high_low(v), 0).astype(jnp.bfloat16)
    twice = jnp.concatenate([constant, constant], 1).astype(jnp.bfloat16)
    return jnp.dot(twice, both, preferred_element_type=jnp.float32)


def speed_parts(speed, left, right):
    ny, nz = left.shape[0] // 3, right.shape[1] // 3
    scale = -STEP_DT * STEP_DT
    rows = spread_left(left, spread_right(speed, right[:, :nz]) * scale)
    cols = spread_right(spread_left(left[:ny], speed) * scale, right[:, nz:])
    return rows[:ny], rows[ny : 2 * ny], rows[2 * ny :], cols[:, :nz], cols[:, nz:]


def halves(v):
    high = v.astype(jnp.bfloat16)
    return high, (v - high.astype(jnp.float32)).astype(jnp.bfloat16)


def split_two(v):
    return jnp.concatenate(halves(v), 1)


def write_pick_z(elem, pick_z):
    slots = elem.shape[1]
    nz = pick_z.shape[0] // 2
    first_z = (elem & (nz // 4 - 1)) * 4
    z_at = lax.broadcasted_iota(jnp.int32, (nz, slots), 0)
    for c in range(5):
        hit = jnp.where(z_at == first_z + c, 1.0, 0.0).astype(jnp.bfloat16)
        pick_z[0:nz, c * slots : (c + 1) * slots] = hit
        pick_z[nz : 2 * nz, c * slots : (c + 1) * slots] = hit


def write_pick_y(elem, weight, layers, pick_y, nz):
    slots = elem.shape[1]
    ny = pick_y.shape[1] // len(layers)
    first_y = (elem >> int(math.log2(nz // 4))) * 4
    y_at = lax.broadcasted_iota(jnp.int32, (ny, slots), 0)
    rows = []
    for b in range(5):
        row = first_y + b
        rows.append(jnp.where(row >= ny, row - ny, row))
    for i, a in enumerate(layers):
        for c in range(5):
            value = jnp.zeros((ny, slots), jnp.float32)
            for b in range(5):
                value = jnp.where(y_at == rows[b], weight(a, b, c), value)
            pick_y[c, i * ny : (i + 1) * ny] = value


def sample(values, pick_z, pick_y):
    rows = values.shape[0]
    slots = pick_y.shape[2]
    total = jnp.zeros((rows, slots), jnp.float32)
    for c in (0, 2, 4):
        some = min(2, 5 - c)
        picked = jnp.dot(
            values,
            pick_z[:, c * slots : (c + some) * slots],
            preferred_element_type=jnp.float32,
        )
        for k in range(some):
            total += picked[:, k * slots : (k + 1) * slots] * pick_y[c + k]
    return jnp.sum(jnp.sum(total.reshape(rows // 8, 8, slots), 0), 0, keepdims=True)


def split_three(v):
    high = v.astype(jnp.bfloat16).astype(jnp.float32)
    rest = v - high
    middle = rest.astype(jnp.bfloat16).astype(jnp.float32)
    return high, middle, rest - middle


def window_kernel(
    axes,
    sizes,
    now_hbm,
    vel_hbm,
    speed_hbm,
    src_hbm,
    elem_hbm,
    weight_hbm,
    left_hbm,
    right_hbm,
    station_hbm,
    along_y_hbm,
    along_z_hbm,
    wave_ref,
    blocks_ref,
    end_hbm,
    picked_ref,
    now_ref,
    vel_ref,
    speed_ref,
    src_ref,
    elem_ref,
    weight_ref,
    left_ref,
    right_ref,
    station_ref,
    along_y,
    along_z,
    field,
    acc,
    coef,
    x_own,
    x_left,
    pick_z,
    pick_y,
    pick_z_left,
    pick_y_left,
    hits,
    samp,
    setup_out,
    setup_in,
    send_v,
    send_p,
    recv_v,
    recv_p,
    recv_v2,
    recv_p2,
    send_a,
    send_b,
    recv_a,
    recv_b,
    send_x,
    x_right,
    x_left2,
    all_samp,
    load_sem,
    ssem,
    rsem,
    pair_ssem,
    pair_rsem,
    setup_sem,
    x_sem,
    all_sem,
    end_sem,
):
    planes, ny, nz = now_ref.shape
    slots = elem_ref.shape[1]
    n = sizes[0] * sizes[1]
    me = lax.axis_index(axes[0]) * sizes[1] + lax.axis_index(axes[1])

    loads = [
        pltpu.make_async_copy(src, dst, load_sem.at[i])
        for i, (src, dst) in enumerate(
            [
                (now_hbm, now_ref),
                (speed_hbm, speed_ref),
                (elem_hbm, elem_ref),
                (weight_hbm, weight_ref),
                (left_hbm, left_ref),
                (right_hbm, right_ref),
                (vel_hbm, vel_ref),
                (src_hbm, src_ref),
                (station_hbm, station_ref),
                (along_y_hbm, along_y),
                (along_z_hbm, along_z),
            ]
        )
    ]
    for load in loads[:4]:
        load.start()

    def device(off):
        j = me + off
        j = jnp.where(j >= n, j - n, j)
        return (lax.div(j, sizes[1]), lax.rem(j, sizes[1]))

    right_dev = device(1)
    left_dev = device(n - 1)
    right_dev2 = device(2)
    left_dev2 = device(n - 2)

    barrier = pltpu.get_barrier_semaphore()

    for off in range(1, n):
        pl.semaphore_signal(barrier, inc=1, device_id=device(off), device_id_type=MESH)
    for load in loads[4:]:
        load.start()

    def to(src, dst, sems, at, target):
        return pltpu.make_async_remote_copy(
            src_ref=src,
            dst_ref=dst,
            send_sem=sems[0].at[at],
            recv_sem=sems[1].at[at],
            device_id=target,
            device_id_type=MESH,
        )

    def copies(t):
        sems = (ssem, rsem)
        return (
            to(send_v.at[t], recv_v.at[t], sems, (0, t), left_dev),
            to(send_p.at[t], recv_p.at[t], sems, (1, t), right_dev),
        )

    def far_copies(t, e):
        sems = (pair_ssem, pair_rsem)
        return (
            to(send_v.at[t], recv_v2.at[e], sems, (0, e), left_dev2),
            to(send_p.at[t], recv_p2.at[e], sems, (1, e), right_dev2),
        )

    def ahead_copies(e):
        sems = (pair_ssem, pair_rsem)
        return (
            to(send_a.at[e], recv_a.at[e], sems, (2, e), left_dev),
            to(send_b.at[e], recv_b.at[e], sems, (3, e), right_dev),
        )

    def x_copies():
        return (
            to(send_x, x_right, (x_sem.at[0], x_sem.at[1]), 0, left_dev),
            to(send_x, x_left2, (x_sem.at[0], x_sem.at[1]), 1, right_dev2),
        )

    def stage(t, u):
        send_v[t] = u[0].astype(jnp.bfloat16)
        total = u[0] * jnp.float32(K1[4, 0])
        for a in range(1, 4):
            total += u[a] * jnp.float32(K1[4, a])
        send_p[t] = total.astype(jnp.bfloat16)

    setup = pltpu.make_async_remote_copy(
        src_ref=setup_out,
        dst_ref=setup_in,
        send_sem=setup_sem.at[0],
        recv_sem=setup_sem.at[1],
        device_id=right_dev,
        device_id_type=MESH,
    )
    ey, ez = ny // 4, nz // 4
    setup_out[...] = jnp.zeros_like(setup_out)
    for load in loads[:4]:
        load.wait()
    elem = elem_ref[...]
    own_speed = speed_ref[0]
    setup_out[0:25] = weight_ref[100:125]
    setup_out[25:26] = elem.astype(jnp.float32)
    setup_out[32 : 32 + ey, 0:ez] = own_speed
    stage(0, [now_ref[p] for p in range(4)])

    pl.semaphore_wait(barrier, n - 1)
    setup.start()
    for copy in copies(0):
        copy.start()

    for load in loads[4:]:
        load.wait()
    for p in range(4):
        value = now_ref[p]
        field[0, p] = value
        field[1, p] = value - STEP_DT * vel_ref[p]
    left = left_ref[...]
    right = right_ref[...]
    own = speed_parts(own_speed, left, right)
    x_own[...] = own[0]
    send_x[...] = own[0].astype(jnp.bfloat16)
    for copy in x_copies():
        copy.start()
    for i in range(4):
        coef[1, i] = own[1 + i]
    write_pick_z(elem, pick_z)
    write_pick_y(
        elem,
        lambda a, b, c: weight_ref[25 * a + 5 * b + c : 25 * a + 5 * b + c + 1, :],
        range(4),
        pick_y,
        nz,
    )
    samp[...] = jnp.zeros_like(samp)

    def partial(t, slot, planes=range(4)):
        drive = wave_ref[t] * jnp.float32(STEP_DT * STEP_DT)
        parts = [halves(field[slot, p]) for p in planes]
        in_y = jnp.dot(
            along_y[...],
            jnp.concatenate([jnp.concatenate([h, l, h], 0) for h, l in parts], 1),
            preferred_element_type=jnp.float32,
        )
        in_z = jnp.dot(
            jnp.concatenate([jnp.concatenate([h, l, h], 1) for h, l in parts], 0),
            along_z[...],
            preferred_element_type=jnp.float32,
        )
        for i, p in enumerate(planes):
            which = 0 if p == 0 else 1
            v = field[slot, p]
            total = 2.0 * v - field[1 - slot, p] + drive * src_ref[p]
            along = field[slot, 0] * jnp.float32(K1[p, 0] / M1[p])
            for a in range(1, 4):
                along += field[slot, a] * jnp.float32(K1[p, a] / M1[p])
            total += x_own[...] * along
            if p == 0:
                total += x_left[...] * (v * jnp.float32(K1[4, 4] / M1[0]))
            columns = slice(i * nz, (i + 1) * nz)
            rows = slice(i * ny, (i + 1) * ny)
            total += coef[which, 0] * in_y[:ny, columns] + coef[which, 1] * in_y[ny:, columns]
            total += coef[which, 2] * in_z[rows, :nz] + coef[which, 3] * in_z[rows, nz:]
            acc[p] = total

    partial(0, 0, range(1, 4))
    setup.wait()
    before = speed_parts(setup_in[32 : 32 + ey, 0:ez], left, right)
    x_left[...] = before[0]
    for i in range(4):
        coef[0, i] = 0.5 * (own[1 + i] + before[1 + i])
    partial(0, 0, range(1))

    def wait_halo(t):
        for copy in copies(t):
            copy.wait_recv()
        return recv_v[t].astype(jnp.float32), recv_p[t].astype(jnp.float32)

    def finish(halo, store):
        far, near = halo
        shared = x_own[...] * far
        out = []
        for p in range(4):
            total = acc[p] + shared * jnp.float32(K1[p, 4] / M1[p])
            if p == 0:
                total += x_left[...] * (near * jnp.float32(1.0 / M1[0]))
            store(p, total)
            out.append(total)
        return out

    def store_in(slot):
        def store(p, value):
            field[slot, p] = value

        return store

    def next_halo(t, e):
        for copy in (*far_copies(t, e), *ahead_copies(e)):
            copy.wait_recv()
        back = sum(K1[4, a] * K1[a, 4] / M1[a] for a in range(4))
        far = (
            recv_a[e].astype(jnp.float32)
            + x_right[...].astype(jnp.float32)
            * (recv_v2[e].astype(jnp.float32) * jnp.float32(K1[0, 4] / M1[0]))
            + x_own[...] * (send_p[t].astype(jnp.float32) * jnp.float32(1.0 / M1[0]))
        )
        near = (
            recv_b[e].astype(jnp.float32)
            + x_left[...] * (field[t % 2, 0] * jnp.float32(back))
            + x_left2[...].astype(jnp.float32)
            * (recv_p2[e].astype(jnp.float32) * jnp.float32(K1[4, 0] / M1[0]))
        )
        return far, near

    def take_samples(t, slot):
        values = jnp.concatenate([split_two(field[slot, p]) for p in range(4)], 0)
        samp[pl.ds(t, 1), :] = sample(values, pick_z, pick_y)
        samp[pl.ds(t + 8, 1), :] = sample(values[:ny], pick_z_left, pick_y_left)

    def two_steps(e, between):
        t = 1 + 2 * e
        for copy in (*copies(t), *far_copies(t, e)):
            copy.start()
        partial(t, 1)
        send_a[e] = acc[0].astype(jnp.bfloat16)
        total = acc[0] * jnp.float32(K1[4, 0])
        for a in range(1, 4):
            total += acc[a] * jnp.float32(K1[4, a])
        send_b[e] = total.astype(jnp.bfloat16)
        for copy in ahead_copies(e):
            copy.start()
        between()
        take_samples(t - 1, 0)
        take_samples(t, 1)
        finish(wait_halo(t), store_in(0))
        halo = next_halo(t, e)
        partial(t + 1, 0)
        stage(t + 2, finish(halo, store_in(1)))

    stage(1, finish(wait_halo(0), store_in(1)))

    def prepare():
        left_elem = setup_in[25:26].astype(jnp.int32)
        write_pick_z(left_elem, pick_z_left)
        write_pick_y(
            left_elem,
            lambda a, b, c: setup_in[5 * b + c : 5 * b + c + 1, :],
            range(4, 5),
            pick_y_left,
            nz,
        )
        for copy in x_copies():
            copy.wait_recv()

    def prepare_hits():
        station = station_ref[...].astype(jnp.float32).T
        k = lax.broadcasted_iota(jnp.int32, (slots, 2 * SB), 1)
        for pair in range(hits.shape[0]):
            first = blocks_ref[pair, 0]
            second = blocks_ref[pair, 1]
            wanted = jnp.where(k < SB, first * SB + k, second * SB + k - SB).astype(jnp.float32)
            for d in range(n):
                hit = jnp.where(wanted == station[:, d : d + 1], 1.0, 0.0)
                hits[pair, d * slots : (d + 1) * slots] = hit.astype(jnp.bfloat16)

    two_steps(0, prepare)
    two_steps(1, prepare_hits)

    last = NT - 1
    slot = last % 2
    for copy in copies(last):
        copy.start()
    take_samples(last - 1, 1 - slot)
    take_samples(last, slot)

    for off in range(1, n):
        pltpu.make_async_remote_copy(
            src_ref=samp,
            dst_ref=all_samp.at[me],
            send_sem=all_sem.at[0],
            recv_sem=all_sem.at[1],
            device_id=device(off),
            device_id_type=MESH,
        ).start()

    partial(last, slot)

    def store_end(p, value):
        acc[p] = value

    finish(wait_halo(last), store_end)
    put_end = pltpu.make_async_copy(acc, end_hbm, end_sem)
    put_end.start()
    whole = all_samp.at[pl.ds(0, n - 1)]
    everyone = pltpu.make_async_remote_copy(
        src_ref=whole,
        dst_ref=whole,
        send_sem=all_sem.at[0],
        recv_sem=all_sem.at[1],
        device_id=right_dev,
        device_id_type=MESH,
    )
    everyone.wait_recv()
    all_samp[me] = samp[...]
    parts = []
    for d in range(n):
        high, middle, low = split_three(all_samp[d, 0:8] + all_samp[(d + 1) % n, 8:16])
        parts.append(jnp.concatenate([high, middle, low, jnp.zeros_like(low)], 0))
    everything = jnp.concatenate(parts, 1).astype(jnp.bfloat16)
    for pair in range(hits.shape[0]):
        picked_ref[pair] = jnp.dot(everything, hits[pair], preferred_element_type=jnp.float32)
    everyone.wait_send()

    put_end.wait()
    for copy in x_copies():
        copy.wait_send()
    for t in (0, 1, 3, 5):
        for copy in copies(t):
            copy.wait_send()
    for e in range(2):
        for copy in (*far_copies(1 + 2 * e, e), *ahead_copies(e)):
            copy.wait_send()


def cross_kernel(picked_hbm, end_ref, table_ref, out_ref, final_ref, waves, picked_ref, held, sem):
    lanes = SB * SB
    pair = pl.program_id(0)
    chunk = pl.program_id(1)
    take = pltpu.make_async_copy(end_ref, held, sem.at[0])
    give = pltpu.make_async_copy(held, final_ref, sem.at[2])

    @pl.when(chunk == 0)
    def _():
        fetch = pltpu.make_async_copy(picked_hbm.at[pair], picked_ref, sem.at[1])
        fetch.start()

        @pl.when(pair == 0)
        def _():
            take.start()

        row = lax.broadcasted_iota(jnp.int32, (2 * SB, 2 * lanes), 0)
        lane = lax.broadcasted_iota(jnp.int32, (2 * SB, 2 * lanes), 1)
        source = jnp.where(lane < lanes, lane // SB, SB + lane % SB)
        spread = jnp.where(row == source, 1.0, 0.0).astype(jnp.bfloat16)
        fetch.wait()
        wide = jnp.dot(
            picked_ref[...].astype(jnp.bfloat16), spread, preferred_element_type=jnp.float32
        )
        high, middle, low = wide[0:8], wide[8:16], wide[16:24]
        waves[...] = jnp.concatenate([high, middle, high, low, high, middle], 0).astype(
            jnp.bfloat16
        )

    def spectrum(part):
        full = jnp.dot(table_ref[part], waves[...], preferred_element_type=jnp.float32)
        full = full.astype(jnp.bfloat16).astype(jnp.float32)
        return full[:, :lanes], full[:, lanes:]

    re_a, re_b = spectrum(0)
    im_a, im_b = spectrum(1)
    out_ref[0, 0] = ((re_a * re_b + im_a * im_b) * jnp.float32(1.0 / NT)).astype(jnp.bfloat16)
    out_ref[0, 1] = ((im_a * re_b - re_a * im_b) * jnp.float32(1.0 / NT)).astype(jnp.bfloat16)

    @pl.when((pair == 0) & (chunk == 0))
    def _():
        take.wait()
        give.start()

    @pl.when((pair == pl.num_programs(0) - 1) & (chunk == pl.num_programs(1) - 1))
    def _():
        give.wait()


def dft_table():
    angle = np.pi * (np.arange(F) + 0.5) / F
    phase = angle[:, None] * np.arange(8)[None, :]
    live = np.arange(8) < NT
    parts = []
    for table in (np.cos(phase) * live, -np.sin(phase) * live):
        table = table.astype(np.float32)
        high = table.astype(jnp.bfloat16).astype(np.float32)
        middle = (table - high).astype(jnp.bfloat16).astype(np.float32)
        low = table - high - middle
        parts.append(np.concatenate([high, high, middle, high, low, middle], 1))
    return jnp.asarray(np.stack(parts).astype(jnp.bfloat16))


def body(axes, sizes, *args):
    now, vel, speed, source, wavelet, elem, station, weight, blocks = args
    planes, ny, nz = now.shape
    slots = elem.shape[0]
    n = sizes[0] * sizes[1]
    pairs = blocks.shape[0]
    left, right = spread_matrices(ny, nz)
    f32, bf16 = jnp.float32, jnp.bfloat16
    anywhere = pl.BlockSpec(memory_space=pl.ANY)
    operands = (
        now,
        vel,
        speed,
        source,
        elem.reshape(1, slots),
        weight,
        jnp.asarray(left),
        jnp.asarray(right),
        station.reshape(n, slots),
        *stencil_matrices(ny, nz),
    )
    end, picked = pl.pallas_call(
        functools.partial(window_kernel, axes, sizes),
        out_shape=(
            jax.ShapeDtypeStruct(now.shape, f32),
            jax.ShapeDtypeStruct((pairs, 32, 2 * SB), f32),
        ),
        in_specs=[anywhere] * len(operands) + [pl.BlockSpec(memory_space=pltpu.SMEM)] * 2,
        out_specs=(anywhere, pl.BlockSpec(memory_space=pltpu.VMEM)),
        scratch_shapes=[pltpu.VMEM(x.shape, x.dtype) for x in operands]
        + [
            pltpu.VMEM((2, planes, ny, nz), f32),
            pltpu.VMEM((planes, ny, nz), f32),
            pltpu.VMEM((2, 4, ny, nz), f32),
            pltpu.VMEM((ny, nz), f32),
            pltpu.VMEM((ny, nz), f32),
            pltpu.VMEM((2 * nz, 5 * slots), bf16),
            pltpu.VMEM((5, planes * ny, slots), f32),
            pltpu.VMEM((2 * nz, 5 * slots), bf16),
            pltpu.VMEM((5, ny, slots), f32),
            pltpu.VMEM((pairs, n * slots, 2 * SB), bf16),
            pltpu.VMEM((16, slots), f32),
            pltpu.VMEM((32 + ny // 4, slots), f32),
            pltpu.VMEM((32 + ny // 4, slots), f32),
            pltpu.VMEM((NT, ny, nz), bf16),
            pltpu.VMEM((NT, ny, nz), bf16),
            pltpu.VMEM((NT, ny, nz), bf16),
            pltpu.VMEM((NT, ny, nz), bf16),
        ]
        + [pltpu.VMEM((2, ny, nz), bf16)] * 6
        + [pltpu.VMEM((ny, nz), bf16)] * 3
        + [
            pltpu.VMEM((n, 16, slots), f32),
            pltpu.SemaphoreType.DMA((len(operands),)),
            pltpu.SemaphoreType.DMA((2, NT)),
            pltpu.SemaphoreType.DMA((2, NT)),
            pltpu.SemaphoreType.DMA((4, 2)),
            pltpu.SemaphoreType.DMA((4, 2)),
            pltpu.SemaphoreType.DMA((2,)),
            pltpu.SemaphoreType.DMA((2, 2)),
            pltpu.SemaphoreType.DMA((2,)),
            pltpu.SemaphoreType.DMA(()),
        ],
        compiler_params=pltpu.CompilerParams(
            collective_id=0, has_side_effects=True, vmem_limit_bytes=56 * 2**20
        ),
        name="window",
    )(*operands, wavelet, blocks)
    chunk = F // 2
    cross, final = pl.pallas_call(
        cross_kernel,
        out_shape=(
            jax.ShapeDtypeStruct((pairs, 2, F, SB * SB), bf16),
            jax.ShapeDtypeStruct(now.shape, f32),
        ),
        grid=(pairs, F // chunk),
        in_specs=[
            anywhere,
            anywhere,
            pl.BlockSpec((2, chunk, 48), lambda p, f: (0, f, 0)),
        ],
        out_specs=(
            pl.BlockSpec((1, 2, chunk, SB * SB), lambda p, f: (p, 0, f, 0)),
            anywhere,
        ),
        scratch_shapes=[
            pltpu.VMEM((48, 2 * SB * SB), bf16),
            pltpu.VMEM((32, 2 * SB), f32),
            pltpu.VMEM(now.shape, f32),
            pltpu.SemaphoreType.DMA((3,)),
        ],
        compiler_params=pltpu.CompilerParams(vmem_limit_bytes=56 * 2**20),
        name="cross",
    )(picked, end, dft_table())
    return final, cross


def solution(mesh):
    axes = ("pair", "bulk")
    sizes = tuple(mesh.shape[a] for a in axes)
    split = P(axes, None, None)
    in_specs = (
        split,
        split,
        split,
        split,
        P(),
        P(axes),
        P(),
        P(None, axes),
        P(axes, None),
    )
    return jax.shard_map(
        functools.partial(body, axes, sizes),
        mesh=mesh,
        in_specs=in_specs,
        out_specs=(split, P(axes, None, None, None)),
        check_vma=False,
    )
```

```python
import functools
import math

import jax
import jax.numpy as jnp
import numpy as np
from jax import lax
from jax.experimental import pallas as pl
from jax.experimental.pallas import tpu as pltpu
from jax.sharding import PartitionSpec as P

NT = 6
F = 256
SB = 32
STEP_DT = 0.04
MESH = pl.DeviceIdType.MESH


def gll_tables():
    points = np.array([-1.0, -math.sqrt(3.0 / 7.0), 0.0, math.sqrt(3.0 / 7.0), 1.0])
    quadrature = np.array([0.1, 49.0 / 90.0, 32.0 / 45.0, 49.0 / 90.0, 0.1])
    factor = np.array(
        [np.prod([points[i] - points[j] for j in range(5) if j != i]) for i in range(5)]
    )
    derivative = np.zeros((5, 5))
    for i in range(5):
        for j in range(5):
            if i != j:
                derivative[i, j] = factor[i] / (factor[j] * (points[i] - points[j]))
        derivative[i, i] = -np.sum(derivative[i])
    return derivative, quadrature


DERIV, QUAD = gll_tables()
K1 = DERIV.T @ np.diag(QUAD) @ DERIV
M1 = np.array([0.2, QUAD[1], QUAD[2], QUAD[3]])


def spread_matrices(ny, nz):
    ey, ez = ny // 4, nz // 4
    wy = np.zeros((ny, ey))
    wz = np.zeros((ez, nz))
    for e in range(ey):
        for b in range(5):
            r = (4 * e + b) % ny
            wy[r, e] += QUAD[b] / M1[r % 4]
    for e in range(ez):
        for c in range(5):
            r = 4 * e + c
            if r < nz:
                wz[e, r] += QUAD[c] / (0.1 if r == 0 else M1[r % 4])
    own_y = np.zeros((ny, ey))
    prev_y = np.zeros((ny, ey))
    own_z = np.zeros((ez, nz))
    prev_z = np.zeros((ez, nz))
    for r in range(ny):
        own_y[r, r // 4] = 1
        prev_y[r, (r // 4 - 1) % ey] = 1
    for c in range(nz):
        own_z[c // 4, c] = 1
        if c >= 4:
            prev_z[c // 4 - 1, c] = 1
    left = np.concatenate([wy, own_y, prev_y], 0).astype(np.float32)
    right = np.concatenate([wz, own_z, prev_z], 1).astype(np.float32)
    return left, right


def own_factor(b, d):
    return K1[b, b + d] / M1[b] if 0 <= b + d <= 4 else 0.0


def prev_factor(b, d):
    return K1[4, 4 + d] / M1[0] if b == 0 and -4 <= d <= 0 else 0.0


def stencil_matrices(ny, nz):
    along_y = np.zeros((2 * ny, ny))
    along_z = np.zeros((nz, 2 * nz))
    for r in range(ny):
        for d in range(-4, 5):
            along_y[r, (r + d) % ny] += own_factor(r % 4, d)
            along_y[ny + r, (r + d) % ny] += prev_factor(r % 4, d)
    for c in range(nz):
        for d in range(-4, 5):
            if 0 <= c + d < nz:
                along_z[c + d, c] += own_factor(c % 4, d) * (M1[0] / 0.1 if c == 0 else 1.0)
                along_z[c + d, nz + c] += prev_factor(c % 4, d) if c >= 4 else 0.0
    out = []
    for matrix, axis in ((along_y, 1), (along_z, 0)):
        matrix = matrix.astype(np.float32)
        high = matrix.astype(jnp.bfloat16)
        low = (matrix - high.astype(np.float32)).astype(jnp.bfloat16)
        out.append(jnp.asarray(np.concatenate([high, high, low], axis)))
    return out


def high_low(v):
    high = v.astype(jnp.bfloat16).astype(jnp.float32)
    return high, v - high


def spread_right(v, constant):
    both = jnp.concatenate(high_low(v), 1).astype(jnp.bfloat16)
    twice = jnp.concatenate([constant, constant], 0).astype(jnp.bfloat16)
    return jnp.dot(both, twice, preferred_element_type=jnp.float32)


def spread_left(constant, v):
    both = jnp.concatenate(high_low(v), 0).astype(jnp.bfloat16)
    twice = jnp.concatenate([constant, constant], 1).astype(jnp.bfloat16)
    return jnp.dot(twice, both, preferred_element_type=jnp.float32)


def speed_parts(speed, left, right):
    ny, nz = left.shape[0] // 3, right.shape[1] // 3
    scale = -STEP_DT * STEP_DT
    rows = spread_left(left, spread_right(speed, right[:, :nz]) * scale)
    cols = spread_right(spread_left(left[:ny], speed) * scale, right[:, nz:])
    return rows[:ny], rows[ny : 2 * ny], rows[2 * ny :], cols[:, :nz], cols[:, nz:]


def halves(v):
    high = v.astype(jnp.bfloat16)
    return high, (v - high.astype(jnp.float32)).astype(jnp.bfloat16)


def split_two(v):
    return jnp.concatenate(halves(v), 1)


def write_pick_z(elem, pick_z):
    slots = elem.shape[1]
    nz = pick_z.shape[0] // 2
    first_z = (elem & (nz // 4 - 1)) * 4
    z_at = lax.broadcasted_iota(jnp.int32, (nz, slots), 0)
    for c in range(5):
        hit = jnp.where(z_at == first_z + c, 1.0, 0.0).astype(jnp.bfloat16)
        pick_z[0:nz, c * slots : (c + 1) * slots] = hit
        pick_z[nz : 2 * nz, c * slots : (c + 1) * slots] = hit


def write_pick_y(elem, weight, layers, pick_y, nz):
    slots = elem.shape[1]
    ny = pick_y.shape[1] // len(layers)
    first_y = (elem >> int(math.log2(nz // 4))) * 4
    y_at = lax.broadcasted_iota(jnp.int32, (ny, slots), 0)
    rows = []
    for b in range(5):
        row = first_y + b
        rows.append(jnp.where(row >= ny, row - ny, row))
    for i, a in enumerate(layers):
        for c in range(5):
            value = jnp.zeros((ny, slots), jnp.float32)
            for b in range(5):
                value = jnp.where(y_at == rows[b], weight(a, b, c), value)
            pick_y[c, i * ny : (i + 1) * ny] = value


def sample(values, pick_z, pick_y):
    rows = values.shape[0]
    slots = pick_y.shape[2]
    total = jnp.zeros((rows, slots), jnp.float32)
    for c in (0, 2, 4):
        some = min(2, 5 - c)
        picked = jnp.dot(
            values,
            pick_z[:, c * slots : (c + some) * slots],
            preferred_element_type=jnp.float32,
        )
        for k in range(some):
            total += picked[:, k * slots : (k + 1) * slots] * pick_y[c + k]
    return jnp.sum(jnp.sum(total.reshape(rows // 8, 8, slots), 0), 0, keepdims=True)


def split_three(v):
    high = v.astype(jnp.bfloat16).astype(jnp.float32)
    rest = v - high
    middle = rest.astype(jnp.bfloat16).astype(jnp.float32)
    return high, middle, rest - middle


def window_kernel(
    axes,
    sizes,
    now_hbm,
    vel_hbm,
    speed_hbm,
    src_hbm,
    elem_hbm,
    weight_hbm,
    left_hbm,
    right_hbm,
    station_hbm,
    along_y_hbm,
    along_z_hbm,
    wave_ref,
    blocks_ref,
    end_hbm,
    picked_ref,
    now_ref,
    vel_ref,
    speed_ref,
    src_ref,
    elem_ref,
    weight_ref,
    left_ref,
    right_ref,
    station_ref,
    along_y,
    along_z,
    field,
    acc,
    coef,
    x_own,
    x_left,
    pick_z,
    pick_y,
    pick_z_left,
    pick_y_left,
    hits,
    samp,
    setup_out,
    setup_in,
    send_v,
    send_p,
    recv_v,
    recv_p,
    recv_v2,
    recv_p2,
    send_a,
    send_b,
    recv_a,
    recv_b,
    send_x,
    x_right,
    x_left2,
    samp_out,
    all_samp,
    load_sem,
    ssem,
    rsem,
    pair_ssem,
    pair_rsem,
    setup_sem,
    x_sem,
    all_sem,
    end_sem,
):
    planes, ny, nz = now_ref.shape
    slots = elem_ref.shape[1]
    n = sizes[0] * sizes[1]
    me = lax.axis_index(axes[0]) * sizes[1] + lax.axis_index(axes[1])

    loads = [
        pltpu.make_async_copy(src, dst, load_sem.at[i])
        for i, (src, dst) in enumerate(
            [
                (now_hbm, now_ref),
                (speed_hbm, speed_ref),
                (elem_hbm, elem_ref),
                (weight_hbm, weight_ref),
                (left_hbm, left_ref),
                (right_hbm, right_ref),
                (vel_hbm, vel_ref),
                (src_hbm, src_ref),
                (station_hbm, station_ref),
                (along_y_hbm, along_y),
                (along_z_hbm, along_z),
            ]
        )
    ]
    for load in loads[:4]:
        load.start()

    def device(off):
        j = me + off
        j = jnp.where(j >= n, j - n, j)
        return (lax.div(j, sizes[1]), lax.rem(j, sizes[1]))

    right_dev = device(1)
    left_dev = device(n - 1)
    right_dev2 = device(2)
    left_dev2 = device(n - 2)

    barrier = pltpu.get_barrier_semaphore()

    for off in range(1, n):
        pl.semaphore_signal(barrier, inc=1, device_id=device(off), device_id_type=MESH)
    for load in loads[4:]:
        load.start()

    def to(src, dst, sems, at, target):
        return pltpu.make_async_remote_copy(
            src_ref=src,
            dst_ref=dst,
            send_sem=sems[0].at[at],
            recv_sem=sems[1].at[at],
            device_id=target,
            device_id_type=MESH,
        )

    def copies(t):
        sems = (ssem, rsem)
        return (
            to(send_v.at[t], recv_v.at[t], sems, (0, t), left_dev),
            to(send_p.at[t], recv_p.at[t], sems, (1, t), right_dev),
        )

    def far_copies(t, e):
        sems = (pair_ssem, pair_rsem)
        return (
            to(send_v.at[t], recv_v2.at[e], sems, (0, e), left_dev2),
            to(send_p.at[t], recv_p2.at[e], sems, (1, e), right_dev2),
        )

    def ahead_copies(e):
        sems = (pair_ssem, pair_rsem)
        return (
            to(send_a.at[e], recv_a.at[e], sems, (2, e), left_dev),
            to(send_b.at[e], recv_b.at[e], sems, (3, e), right_dev),
        )

    def x_copies():
        return (
            to(send_x, x_right, (x_sem.at[0], x_sem.at[1]), 0, left_dev),
            to(send_x, x_left2, (x_sem.at[0], x_sem.at[1]), 1, right_dev2),
        )

    def stage(t, u):
        send_v[t] = u[0].astype(jnp.bfloat16)
        total = u[0] * jnp.float32(K1[4, 0])
        for a in range(1, 4):
            total += u[a] * jnp.float32(K1[4, a])
        send_p[t] = total.astype(jnp.bfloat16)

    setup = pltpu.make_async_remote_copy(
        src_ref=setup_out,
        dst_ref=setup_in,
        send_sem=setup_sem.at[0],
        recv_sem=setup_sem.at[1],
        device_id=right_dev,
        device_id_type=MESH,
    )
    ey, ez = ny // 4, nz // 4
    setup_out[...] = jnp.zeros_like(setup_out)
    for load in loads[:4]:
        load.wait()
    elem = elem_ref[...]
    own_speed = speed_ref[0]
    setup_out[0:25] = weight_ref[100:125]
    setup_out[25:26] = elem.astype(jnp.float32)
    setup_out[32 : 32 + ey, 0:ez] = own_speed
    stage(0, [now_ref[p] for p in range(4)])

    pl.semaphore_wait(barrier, n - 1)
    setup.start()
    for copy in copies(0):
        copy.start()

    for load in loads[4:]:
        load.wait()
    for p in range(4):
        value = now_ref[p]
        field[0, p] = value
        field[1, p] = value - STEP_DT * vel_ref[p]
    left = left_ref[...]
    right = right_ref[...]
    own = speed_parts(own_speed, left, right)
    x_own[...] = own[0]
    send_x[...] = own[0].astype(jnp.bfloat16)
    for copy in x_copies():
        copy.start()
    for i in range(4):
        coef[1, i] = own[1 + i]
    write_pick_z(elem, pick_z)
    write_pick_y(
        elem,
        lambda a, b, c: weight_ref[25 * a + 5 * b + c : 25 * a + 5 * b + c + 1, :],
        range(4),
        pick_y,
        nz,
    )
    samp[...] = jnp.zeros_like(samp)

    def partial(t, slot, planes=range(4)):
        drive = wave_ref[t] * jnp.float32(STEP_DT * STEP_DT)
        parts = [halves(field[slot, p]) for p in planes]
        in_y = jnp.dot(
            along_y[...],
            jnp.concatenate([jnp.concatenate([h, l, h], 0) for h, l in parts], 1),
            preferred_element_type=jnp.float32,
        )
        in_z = jnp.dot(
            jnp.concatenate([jnp.concatenate([h, l, h], 1) for h, l in parts], 0),
            along_z[...],
            preferred_element_type=jnp.float32,
        )
        for i, p in enumerate(planes):
            which = 0 if p == 0 else 1
            v = field[slot, p]
            total = 2.0 * v - field[1 - slot, p] + drive * src_ref[p]
            along = field[slot, 0] * jnp.float32(K1[p, 0] / M1[p])
            for a in range(1, 4):
                along += field[slot, a] * jnp.float32(K1[p, a] / M1[p])
            total += x_own[...] * along
            if p == 0:
                total += x_left[...] * (v * jnp.float32(K1[4, 4] / M1[0]))
            columns = slice(i * nz, (i + 1) * nz)
            rows = slice(i * ny, (i + 1) * ny)
            total += coef[which, 0] * in_y[:ny, columns] + coef[which, 1] * in_y[ny:, columns]
            total += coef[which, 2] * in_z[rows, :nz] + coef[which, 3] * in_z[rows, nz:]
            acc[p] = total

    partial(0, 0, range(1, 4))
    setup.wait()
    before = speed_parts(setup_in[32 : 32 + ey, 0:ez], left, right)
    x_left[...] = before[0]
    for i in range(4):
        coef[0, i] = 0.5 * (own[1 + i] + before[1 + i])
    partial(0, 0, range(1))

    def wait_halo(t):
        for copy in copies(t):
            copy.wait_recv()
        return recv_v[t].astype(jnp.float32), recv_p[t].astype(jnp.float32)

    def finish(halo, store):
        far, near = halo
        shared = x_own[...] * far
        out = []
        for p in range(4):
            total = acc[p] + shared * jnp.float32(K1[p, 4] / M1[p])
            if p == 0:
                total += x_left[...] * (near * jnp.float32(1.0 / M1[0]))
            store(p, total)
            out.append(total)
        return out

    def store_in(slot):
        def store(p, value):
            field[slot, p] = value

        return store

    def next_halo(t, e):
        for copy in (*far_copies(t, e), *ahead_copies(e)):
            copy.wait_recv()
        back = sum(K1[4, a] * K1[a, 4] / M1[a] for a in range(4))
        far = (
            recv_a[e].astype(jnp.float32)
            + x_right[...].astype(jnp.float32)
            * (recv_v2[e].astype(jnp.float32) * jnp.float32(K1[0, 4] / M1[0]))
            + x_own[...] * (send_p[t].astype(jnp.float32) * jnp.float32(1.0 / M1[0]))
        )
        near = (
            recv_b[e].astype(jnp.float32)
            + x_left[...] * (field[t % 2, 0] * jnp.float32(back))
            + x_left2[...].astype(jnp.float32)
            * (recv_p2[e].astype(jnp.float32) * jnp.float32(K1[4, 0] / M1[0]))
        )
        return far, near

    def take_samples(t, slot):
        values = jnp.concatenate([split_two(field[slot, p]) for p in range(4)], 0)
        samp[pl.ds(t, 1), :] = sample(values, pick_z, pick_y)
        samp[pl.ds(t + 8, 1), :] = sample(values[:ny], pick_z_left, pick_y_left)

    def two_steps(e, between):
        t = 1 + 2 * e
        for copy in (*copies(t), *far_copies(t, e)):
            copy.start()
        partial(t, 1)
        send_a[e] = acc[0].astype(jnp.bfloat16)
        total = acc[0] * jnp.float32(K1[4, 0])
        for a in range(1, 4):
            total += acc[a] * jnp.float32(K1[4, a])
        send_b[e] = total.astype(jnp.bfloat16)
        for copy in ahead_copies(e):
            copy.start()
        between()
        take_samples(t - 1, 0)
        take_samples(t, 1)
        finish(wait_halo(t), store_in(0))
        halo = next_halo(t, e)
        partial(t + 1, 0)
        stage(t + 2, finish(halo, store_in(1)))

    stage(1, finish(wait_halo(0), store_in(1)))

    def prepare():
        left_elem = setup_in[25:26].astype(jnp.int32)
        write_pick_z(left_elem, pick_z_left)
        write_pick_y(
            left_elem,
            lambda a, b, c: setup_in[5 * b + c : 5 * b + c + 1, :],
            range(4, 5),
            pick_y_left,
            nz,
        )
        for copy in x_copies():
            copy.wait_recv()

    def prepare_hits():
        station = station_ref[...].astype(jnp.float32).T
        k = lax.broadcasted_iota(jnp.int32, (slots, 2 * SB), 1)
        for pair in range(hits.shape[0]):
            first = blocks_ref[pair, 0]
            second = blocks_ref[pair, 1]
            wanted = jnp.where(k < SB, first * SB + k, second * SB + k - SB).astype(jnp.float32)
            for d in range(n):
                hit = jnp.where(wanted == station[:, d : d + 1], 1.0, 0.0)
                hits[pair, d * slots : (d + 1) * slots] = hit.astype(jnp.bfloat16)

    two_steps(0, prepare)
    two_steps(1, prepare_hits)

    last = NT - 1
    slot = last % 2
    for copy in copies(last):
        copy.start()
    take_samples(last - 1, 1 - slot)
    take_samples(last, slot)
    samp_out[...] = samp[...].astype(jnp.bfloat16)

    for off in range(1, n):
        pltpu.make_async_remote_copy(
            src_ref=samp_out,
            dst_ref=all_samp.at[me],
            send_sem=all_sem.at[0],
            recv_sem=all_sem.at[1],
            device_id=device(off),
            device_id_type=MESH,
        ).start()

    partial(last, slot)

    def store_end(p, value):
        acc[p] = value

    finish(wait_halo(last), store_end)
    put_end = pltpu.make_async_copy(acc, end_hbm, end_sem)
    put_end.start()
    whole = all_samp.at[pl.ds(0, n - 1)]
    everyone = pltpu.make_async_remote_copy(
        src_ref=whole,
        dst_ref=whole,
        send_sem=all_sem.at[0],
        recv_sem=all_sem.at[1],
        device_id=right_dev,
        device_id_type=MESH,
    )
    everyone.wait_recv()
    all_samp[me] = samp_out[...]
    blocks = [all_samp[d].astype(jnp.float32) for d in range(n)]
    parts = []
    for d in range(n):
        high, middle, low = split_three(blocks[d][0:8] + blocks[(d + 1) % n][8:16])
        parts.append(jnp.concatenate([high, middle, low, jnp.zeros_like(low)], 0))
    everything = jnp.concatenate(parts, 1).astype(jnp.bfloat16)
    for pair in range(hits.shape[0]):
        picked_ref[pair] = jnp.dot(everything, hits[pair], preferred_element_type=jnp.float32)
    everyone.wait_send()

    put_end.wait()
    for copy in x_copies():
        copy.wait_send()
    for t in (0, 1, 3, 5):
        for copy in copies(t):
            copy.wait_send()
    for e in range(2):
        for copy in (*far_copies(1 + 2 * e, e), *ahead_copies(e)):
            copy.wait_send()


def cross_kernel(picked_ref, end_ref, table_ref, out_ref, final_ref, waves, held, sem):
    lanes = SB * SB
    pair = pl.program_id(0)
    chunk = pl.program_id(1)
    take = pltpu.make_async_copy(end_ref, held, sem.at[0])
    give = pltpu.make_async_copy(held, final_ref, sem.at[2])

    @pl.when(chunk == 0)
    def _():
        @pl.when(pair == 0)
        def _():
            take.start()

        row = lax.broadcasted_iota(jnp.int32, (2 * SB, 2 * lanes), 0)
        lane = lax.broadcasted_iota(jnp.int32, (2 * SB, 2 * lanes), 1)
        source = jnp.where(lane < lanes, lane // SB, SB + lane % SB)
        spread = jnp.where(row == source, 1.0, 0.0).astype(jnp.bfloat16)
        wide = jnp.dot(
            picked_ref[0].astype(jnp.bfloat16), spread, preferred_element_type=jnp.float32
        )
        high, middle, low = wide[0:8], wide[8:16], wide[16:24]
        waves[...] = jnp.concatenate([high, middle, high, low, high, middle], 0).astype(
            jnp.bfloat16
        )

    rows = table_ref.shape[1]
    table = table_ref[...].reshape(2 * rows, table_ref.shape[2])
    full = jnp.dot(table, waves[...], preferred_element_type=jnp.float32)
    full = full.astype(jnp.bfloat16).astype(jnp.float32)
    re_a, re_b = full[:rows, :lanes], full[:rows, lanes:]
    im_a, im_b = full[rows:, :lanes], full[rows:, lanes:]
    out_ref[0, 0] = ((re_a * re_b + im_a * im_b) * jnp.float32(1.0 / NT)).astype(jnp.bfloat16)
    out_ref[0, 1] = ((im_a * re_b - re_a * im_b) * jnp.float32(1.0 / NT)).astype(jnp.bfloat16)

    @pl.when((pair == 0) & (chunk == 0))
    def _():
        take.wait()
        give.start()

    @pl.when((pair == pl.num_programs(0) - 1) & (chunk == pl.num_programs(1) - 1))
    def _():
        give.wait()


def dft_table():
    angle = np.pi * (np.arange(F) + 0.5) / F
    phase = angle[:, None] * np.arange(8)[None, :]
    live = np.arange(8) < NT
    parts = []
    for table in (np.cos(phase) * live, -np.sin(phase) * live):
        table = table.astype(np.float32)
        high = table.astype(jnp.bfloat16).astype(np.float32)
        middle = (table - high).astype(jnp.bfloat16).astype(np.float32)
        low = table - high - middle
        parts.append(np.concatenate([high, high, middle, high, low, middle], 1))
    return jnp.asarray(np.stack(parts).astype(jnp.bfloat16))


def body(axes, sizes, *args):
    now, vel, speed, source, wavelet, elem, station, weight, blocks = args
    planes, ny, nz = now.shape
    slots = elem.shape[0]
    n = sizes[0] * sizes[1]
    pairs = blocks.shape[0]
    left, right = spread_matrices(ny, nz)
    f32, bf16 = jnp.float32, jnp.bfloat16
    anywhere = pl.BlockSpec(memory_space=pl.ANY)
    operands = (
        now,
        vel,
        speed,
        source,
        elem.reshape(1, slots),
        weight,
        jnp.asarray(left),
        jnp.asarray(right),
        station.reshape(n, slots),
        *stencil_matrices(ny, nz),
    )
    end, picked = pl.pallas_call(
        functools.partial(window_kernel, axes, sizes),
        out_shape=(
            jax.ShapeDtypeStruct(now.shape, f32),
            jax.ShapeDtypeStruct((pairs, 32, 2 * SB), f32),
        ),
        in_specs=[anywhere] * len(operands) + [pl.BlockSpec(memory_space=pltpu.SMEM)] * 2,
        out_specs=(anywhere, pl.BlockSpec(memory_space=pltpu.VMEM)),
        scratch_shapes=[pltpu.VMEM(x.shape, x.dtype) for x in operands]
        + [
            pltpu.VMEM((2, planes, ny, nz), f32),
            pltpu.VMEM((planes, ny, nz), f32),
            pltpu.VMEM((2, 4, ny, nz), f32),
            pltpu.VMEM((ny, nz), f32),
            pltpu.VMEM((ny, nz), f32),
            pltpu.VMEM((2 * nz, 5 * slots), bf16),
            pltpu.VMEM((5, planes * ny, slots), f32),
            pltpu.VMEM((2 * nz, 5 * slots), bf16),
            pltpu.VMEM((5, ny, slots), f32),
            pltpu.VMEM((pairs, n * slots, 2 * SB), bf16),
            pltpu.VMEM((16, slots), f32),
            pltpu.VMEM((32 + ny // 4, slots), f32),
            pltpu.VMEM((32 + ny // 4, slots), f32),
            pltpu.VMEM((NT, ny, nz), bf16),
            pltpu.VMEM((NT, ny, nz), bf16),
            pltpu.VMEM((NT, ny, nz), bf16),
            pltpu.VMEM((NT, ny, nz), bf16),
        ]
        + [pltpu.VMEM((2, ny, nz), bf16)] * 6
        + [pltpu.VMEM((ny, nz), bf16)] * 3
        + [
            pltpu.VMEM((16, slots), bf16),
            pltpu.VMEM((n, 16, slots), bf16),
            pltpu.SemaphoreType.DMA((len(operands),)),
            pltpu.SemaphoreType.DMA((2, NT)),
            pltpu.SemaphoreType.DMA((2, NT)),
            pltpu.SemaphoreType.DMA((4, 2)),
            pltpu.SemaphoreType.DMA((4, 2)),
            pltpu.SemaphoreType.DMA((2,)),
            pltpu.SemaphoreType.DMA((2, 2)),
            pltpu.SemaphoreType.DMA((2,)),
            pltpu.SemaphoreType.DMA(()),
        ],
        compiler_params=pltpu.CompilerParams(
            collective_id=0, has_side_effects=True, vmem_limit_bytes=56 * 2**20
        ),
        name="window",
    )(*operands, wavelet, blocks)
    chunk = F // 2
    cross, final = pl.pallas_call(
        cross_kernel,
        out_shape=(
            jax.ShapeDtypeStruct((pairs, 2, F, SB * SB), bf16),
            jax.ShapeDtypeStruct(now.shape, f32),
        ),
        grid=(pairs, F // chunk),
        in_specs=[
            pl.BlockSpec((1, 32, 2 * SB), lambda p, f: (p, 0, 0)),
            anywhere,
            pl.BlockSpec((2, chunk, 48), lambda p, f: (0, f, 0)),
        ],
        out_specs=(
            pl.BlockSpec((1, 2, chunk, SB * SB), lambda p, f: (p, 0, f, 0)),
            anywhere,
        ),
        scratch_shapes=[
            pltpu.VMEM((48, 2 * SB * SB), bf16),
            pltpu.VMEM(now.shape, f32),
            pltpu.SemaphoreType.DMA((3,)),
        ],
        compiler_params=pltpu.CompilerParams(vmem_limit_bytes=56 * 2**20),
        name="cross",
    )(picked, end, dft_table())
    return final, cross


def solution(mesh):
    axes = ("pair", "bulk")
    sizes = tuple(mesh.shape[a] for a in axes)
    split = P(axes, None, None)
    in_specs = (
        split,
        split,
        split,
        split,
        P(),
        P(axes),
        P(),
        P(None, axes),
        P(axes, None),
    )
    return jax.shard_map(
        functools.partial(body, axes, sizes),
        mesh=mesh,
        in_specs=in_specs,
        out_specs=(split, P(axes, None, None, None)),
        check_vma=False,
    )
```
